32 devices in a mesh: row: 4 (over y, x), col: 8 (over z, core).
Axes of the slice: x: 2, y: 2, z: 4, core: 2. Of those that a mesh axis runs over, the one named last changes fastest.
Arguments:
- query: bfloat16 [1024, 1024], P(('row', 'col')), may hold values from -0.5375 to 0.5375
- passage: bfloat16 [1024, 1024], P(('row', 'col')), may hold values from -0.43 to 0.43
- positive: int32 [32, 32], P(('row', 'col')), may hold values from 0 to 31, each once within a row
Outputs:
- loss_value: float32 [], replicated
- grad_query: bfloat16 [1024, 1024], P(('row', 'col'))
- grad_passage: bfloat16 [1024, 1024], P(('row', 'col'))
The draws below stay inside these ranges and needn't reach their ends.
Inputs may be any that keep to these rules, and one draw needn't show every extreme that they name: Each row of positive names every position 0 to 31 once.
All inputs are finite; a program needn't handle non-finite values.
Results may differ from the reference program's by a relative error of at most 0.015.
Values may be sent and summed in bfloat16 or wider, within the bound.
A program may use at most 64 MiB of HBM per device.

```python
import jax
import jax.numpy as jnp
from jax import lax

EMBED = 1024
ROWS_DEV = 32
BLOCKS = 32
BATCH = 1024
N_ROW = 4
N_COL = 8


emb_scale = 0.07


def drawn_rows(key):
    row_index = jnp.arange(BATCH, dtype=jnp.int32)
    shard_index = row_index // ROWS_DEV
    pattern = jax.random.uniform(jax.random.fold_in(key, 37), (BATCH, EMBED), jnp.float32, -1.0, 1.0)
    level = 150.0 + 80.0 * (shard_index % 2).astype(jnp.float32) + 10.0 * (shard_index // 2 % 3).astype(jnp.float32)
    amplitude = jnp.sqrt(level * 3.0 / (20.0 * EMBED))
    return (row_index, pattern, amplitude)


def draw_passage(key, part):
    subkey = jax.random.fold_in(key, 11)
    values = jax.random.truncated_normal(subkey, -6.0, 6.0, (BATCH, EMBED), jnp.float32) * emb_scale
    row_index, pattern, amplitude = drawn_rows(key)
    own_aligned = row_index % ROWS_DEV == 0
    partner_aligned = row_index % ROWS_DEV == 1
    own_values = amplitude[:, None] * pattern
    partner_values = 0.99 * own_values[row_index ^ 1]
    values = jnp.where(own_aligned[:, None], own_values, jnp.where(partner_aligned[:, None], partner_values, values))
    return values.astype(jnp.bfloat16)


def draw_query(key, part):
    subkey = jax.random.fold_in(key, 23)
    row_index, pattern, amplitude = drawn_rows(key)
    shard_index = row_index // ROWS_DEV
    shard_pos = shard_index.astype(jnp.float32) / (BLOCKS - 1.0)
    parity = (shard_index % 2).astype(jnp.float32)
    spread = (1.0 + 2.0 * shard_pos) * (1.0 + parity)
    sigma = spread / (20.0 * emb_scale * jnp.sqrt(EMBED * 1.0))
    values = jax.random.truncated_normal(subkey, -4.0, 4.0, (BATCH, EMBED), jnp.float32) * sigma[:, None]
    aligned = row_index % ROWS_DEV == 0
    values = jnp.where(aligned[:, None], amplitude[:, None] * pattern, values)
    return values.astype(jnp.bfloat16)


def setup_inputs(seed: int = 0) -> dict:
    key_of = jax.random.split(jax.random.key(seed), 4)
    return {
        "query": draw_query(jax.random.fold_in(key_of[3], 71), 0),
        "passage": draw_passage(jax.random.fold_in(key_of[3], 71), 0),
        "positive": jax.vmap(lambda own: jax.random.permutation(own, ROWS_DEV))(jax.random.split(key_of[2], BLOCKS)).reshape((BLOCKS, ROWS_DEV)).astype(jnp.int32),
    }


logit_scale = 20.0


def reference(query, passage, positive):
    paired_index = (jnp.arange(BLOCKS, dtype=jnp.int32)[:, None] * ROWS_DEV + positive.astype(jnp.int32)).reshape(BATCH)
    query_groups = query.reshape(N_ROW, N_COL * ROWS_DEV, EMBED)
    passage_groups = passage.reshape(N_ROW, N_COL, ROWS_DEV, EMBED).transpose(1, 0, 2, 3).reshape(N_COL, N_ROW * ROWS_DEV, EMBED)

    def tile_scores(query_rows):
        return logit_scale * jnp.dot(query_rows, passage.T, preferred_element_type=jnp.float32)

    def first_sweep(carry, query_rows):
        old_peak, old_total = carry
        scores = tile_scores(query_rows)
        row_lse = jax.nn.logsumexp(scores, axis=1)
        new_peak = jnp.maximum(old_peak, scores.max(axis=0))
        new_total = old_total * jnp.exp(old_peak - new_peak) + jnp.exp(scores - new_peak[None, :]).sum(axis=0)
        return (new_peak, new_total), row_lse

    start_peak = jnp.full((BATCH,), -1e30, jnp.float32)
    start_total = jnp.zeros((BATCH,), jnp.float32)
    (col_peak, col_total), row_lse = lax.scan(first_sweep, (start_peak, start_total), query_groups)
    col_lse = col_peak + jnp.log(col_total)

    def second_sweep(passage_acc, inputs):
        query_rows, row_part = inputs
        scores = tile_scores(query_rows)
        weights = (0.5 * (jnp.exp(scores - row_part[:, None]) + jnp.exp(scores - col_lse[None, :]))).astype(jnp.bfloat16)
        grouped = weights.reshape(-1, N_ROW, N_COL, ROWS_DEV).transpose(2, 0, 1, 3).reshape(N_COL, -1, N_ROW * ROWS_DEV)
        partials = jnp.einsum("cik,ckd->cid", grouped.astype(jnp.float32), passage_groups.astype(jnp.float32), precision=lax.Precision.HIGHEST)
        partials = lax.optimization_barrier(partials.astype(jnp.bfloat16)).astype(jnp.float32)
        query_part = partials.sum(axis=0)
        passage_part = jnp.dot(weights.T, query_rows, preferred_element_type=jnp.float32)
        passage_part = lax.optimization_barrier(passage_part.astype(jnp.bfloat16)).astype(jnp.float32)
        return passage_acc + passage_part, query_part

    passage_sum, query_sums = lax.scan(second_sweep, jnp.zeros((BATCH, EMBED), jnp.float32), (query_groups, row_lse))
    query_sum = query_sums.reshape(BATCH, EMBED)
    row_lse = row_lse.reshape(BATCH)
    paired_passage = passage[paired_index].astype(jnp.float32)
    positive_score = logit_scale * jnp.sum(query.astype(jnp.float32) * paired_passage, axis=1)
    loss_value = (jnp.sum(row_lse) + jnp.sum(col_lse) - 2.0 * jnp.sum(positive_score)) / (2.0 * BATCH)
    grad_query = (logit_scale * (query_sum - paired_passage)).astype(jnp.bfloat16)
    paired_query = jnp.zeros((BATCH, EMBED), jnp.float32).at[paired_index].set(query.astype(jnp.float32))
    grad_passage = (logit_scale * (passage_sum - paired_query)).astype(jnp.bfloat16)
    return (loss_value, grad_query, grad_passage)
```

```python
import functools

import jax
import jax.numpy as jnp
from jax import lax
from jax.experimental import pallas as pl
from jax.experimental.pallas import tpu as pltpu
from jax.sharding import PartitionSpec as P

logit_scale = 20.0
MESH = pl.DeviceIdType.MESH
F32 = jnp.float32
BF16 = jnp.bfloat16
NT = (((1,), (1,)), ((), ()))
TN = (((0,), (0,)), ((), ()))


def kernel(
    n_row, n_col, q_ref, p_ref, pos_ref, loss_ref, gq_ref, gp_ref,
    q_all, p_all, pos_v, pair_p, pair_q, row_stat, col_stat,
    dq_send, dp_send, dq_recv, dp_recv, loss_g, loss_z,
    local_sem, q_ss, q_rs, p_ss, p_rs, rst_ss, rst_rs, cst_ss, cst_rs,
    dq_ss, dq_rs, dp_ss, dp_rs, lg_ss, lg_rs, lz_ss, lz_rs,
):
    rows, width = q_ref.shape
    n_z = n_col // 2
    n_g = n_row * 2
    n_q = n_z * rows
    n_p = n_g * rows
    r = lax.axis_index("row")
    c = lax.axis_index("col")
    z = c // 2
    core = c % 2
    g = r * 2 + core

    def z_dev(d):
        zz = lax.rem(z + d, n_z)
        return zz, (r, zz * 2 + core)

    def g_dev(d):
        gg = lax.rem(g + d, n_g)
        return gg, (gg // 2, z * 2 + gg % 2)

    def z_copy(d, src, dst, ss, rs):
        return pltpu.make_async_remote_copy(
            src_ref=src, dst_ref=dst, send_sem=ss.at[d], recv_sem=rs.at[d],
            device_id=z_dev(d)[1], device_id_type=MESH)

    def g_copy(d, src, dst, ss, rs):
        return pltpu.make_async_remote_copy(
            src_ref=src, dst_ref=dst, send_sem=ss.at[d], recv_sem=rs.at[d],
            device_id=g_dev(d)[1], device_id_type=MESH)

    z_range = range(1, n_z)
    g_range = range(1, n_g)

    own_p = pltpu.make_async_copy(p_ref, p_all.at[g], local_sem.at[0])
    own_q = pltpu.make_async_copy(q_ref, q_all.at[z], local_sem.at[1])
    own_pos = pltpu.make_async_copy(pos_ref, pos_v, local_sem.at[2])
    own_p.start()
    own_q.start()
    own_pos.start()

    barrier = pltpu.get_barrier_semaphore()
    for d in z_range:
        pl.semaphore_signal(barrier, inc=1, device_id=z_dev(d)[1], device_id_type=MESH)
    for d in g_range:
        pl.semaphore_signal(barrier, inc=1, device_id=g_dev(d)[1], device_id_type=MESH)
    pl.semaphore_wait(barrier, n_z - 1 + n_g - 1)

    q_copies = [z_copy(d, q_ref, q_all.at[z], q_ss, q_rs) for d in z_range]
    p_copies = [g_copy(d, p_ref, p_all.at[g], p_ss, p_rs) for d in g_range]
    for cp in q_copies:
        cp.start()
    for cp in p_copies:
        cp.start()

    own_p.wait()
    own_q.wait()
    own_pos.wait()
    q_own = q_all[z]
    p_own = p_all[g]
    slot = lax.broadcasted_iota(jnp.int32, (rows, rows), 0)
    onehot_t = jnp.where(slot == pos_v[...], 1.0, 0.0).astype(F32)
    paired_p = jnp.dot(onehot_t.T.astype(BF16), p_own, preferred_element_type=F32)
    pair_p[...] = paired_p
    pair_q[...] = jnp.dot(onehot_t.astype(BF16), q_own, preferred_element_type=F32)
    pos_sum = logit_scale * jnp.sum(q_own.astype(F32) * paired_p, axis=(0, 1), keepdims=True)

    for cp in q_copies:
        cp.wait()
    for cp in p_copies:
        cp.wait()

    q_mat = q_all[...].reshape(n_q, width)
    p_mat = p_all[...].reshape(n_p, width)
    s = logit_scale * lax.dot_general(q_mat, p_mat, NT, preferred_element_type=F32)
    s_t = logit_scale * lax.dot_general(p_mat, q_mat, NT, preferred_element_type=F32)

    col_peak = jnp.max(s, axis=0, keepdims=True)
    col_sum = jnp.sum(jnp.exp(s - col_peak), axis=0, keepdims=True)
    col_stat[g, 0:1, :] = col_peak
    col_stat[g, 1:2, :] = col_sum
    cst = [g_copy(d, col_stat.at[g], col_stat.at[g], cst_ss, cst_rs) for d in g_range]
    for cp in cst:
        cp.start()
    row_peak = jnp.max(s_t, axis=0, keepdims=True)
    row_sum = jnp.sum(jnp.exp(s_t - row_peak), axis=0, keepdims=True)
    row_stat[z, 0:1, :] = row_peak
    row_stat[z, 1:2, :] = row_sum
    row_stat[z, 2:3, :] = jnp.broadcast_to(pos_sum, (1, n_q))
    rst = [z_copy(d, row_stat.at[z], row_stat.at[z], rst_ss, rst_rs) for d in z_range]
    for cp in rst:
        cp.start()
    for cp in rst:
        cp.wait()
    for cp in cst:
        cp.wait()

    def merge(ref):
        peak = ref[:, 0, :]
        total = ref[:, 1, :]
        top = jnp.max(peak, axis=0, keepdims=True)
        return top + jnp.log(jnp.sum(total * jnp.exp(peak - top), axis=0, keepdims=True))

    row_lse = merge(row_stat)
    col_lse = merge(col_stat)
    pos_group = jnp.sum(row_stat[:, 2, 0:1], axis=0, keepdims=True)
    loss_g[g] = jnp.broadcast_to(jnp.sum(row_lse, axis=1, keepdims=True) - 2.0 * pos_group, (8, 128))
    loss_z[z] = jnp.broadcast_to(jnp.sum(col_lse, axis=1, keepdims=True), (8, 128))

    row_mat = jnp.broadcast_to(row_lse, (128, n_q)).T
    row_mat = jnp.concatenate([row_mat] * (n_p // 128), axis=1)
    w = (0.5 * (jnp.exp(s - row_mat) + jnp.exp(s - col_lse))).astype(BF16)

    dq = jnp.dot(w, p_mat, preferred_element_type=F32).astype(BF16)
    dq_send[...] = dq.reshape(n_z, rows, width)
    dqc = [z_copy(d, dq_send.at[z_dev(d)[0]], dq_recv.at[z], dq_ss, dq_rs) for d in z_range]
    lzc = [z_copy(d, loss_z.at[z], loss_z.at[z], lz_ss, lz_rs) for d in z_range]
    for cp in dqc + lzc:
        cp.start()
    dp = lax.dot_general(w, q_mat, TN, preferred_element_type=F32).astype(BF16)
    dp_send[...] = dp.reshape(n_g, rows, width)
    dpc = [g_copy(d, dp_send.at[g_dev(d)[0]], dp_recv.at[g], dp_ss, dp_rs) for d in g_range]
    lgc = [g_copy(d, loss_g.at[g], loss_g.at[g], lg_ss, lg_rs) for d in g_range]
    for cp in dpc + lgc:
        cp.start()
    dq_recv[z] = dq_send[z]
    dp_recv[g] = dp_send[g]

    for cp in lzc + lgc:
        cp.wait()
    total = jnp.sum(loss_g[:, 0, 0:1], axis=0, keepdims=True) + jnp.sum(loss_z[:, 0, 0:1], axis=0, keepdims=True)
    loss_ref[...] = total / (2.0 * rows * n_row * n_col)

    for cp in dpc:
        cp.wait()
    acc = dp_recv[0].astype(F32)
    for i in range(1, n_g):
        acc += dp_recv[i].astype(F32)
    gp_ref[...] = (logit_scale * (acc - pair_q[...])).astype(BF16)
    for cp in dqc:
        cp.wait()
    acc = dq_recv[0].astype(F32)
    for i in range(1, n_z):
        acc += dq_recv[i].astype(F32)
    gq_ref[...] = (logit_scale * (acc - pair_p[...])).astype(BF16)


def local(n_row, n_col, query, passage, positive):
    rows, width = query.shape
    n_z, n_g = n_col // 2, n_row * 2
    n_q, n_p = n_z * rows, n_g * rows
    dma = pltpu.SemaphoreType.DMA
    loss, gq, gp = pl.pallas_call(
        functools.partial(kernel, n_row, n_col),
        out_shape=(
            jax.ShapeDtypeStruct((1, 1), F32),
            jax.ShapeDtypeStruct((rows, width), BF16),
            jax.ShapeDtypeStruct((rows, width), BF16),
        ),
        in_specs=[pl.BlockSpec(memory_space=pl.ANY)] * 3,
        out_specs=[pl.BlockSpec(memory_space=pltpu.VMEM)] * 3,
        scratch_shapes=[
            pltpu.VMEM((n_z, rows, width), BF16),
            pltpu.VMEM((n_g, rows, width), BF16),
            pltpu.VMEM((1, rows), jnp.int32),
            pltpu.VMEM((rows, width), F32),
            pltpu.VMEM((rows, width), F32),
            pltpu.VMEM((n_z, 8, n_q), F32),
            pltpu.VMEM((n_g, 8, n_p), F32),
            pltpu.VMEM((n_z, rows, width), BF16),
            pltpu.VMEM((n_g, rows, width), BF16),
            pltpu.VMEM((n_z, rows, width), BF16),
            pltpu.VMEM((n_g, rows, width), BF16),
            pltpu.VMEM((n_g, 8, 128), F32),
            pltpu.VMEM((n_z, 8, 128), F32),
            dma((3,)),
            dma((n_z,)), dma((n_z,)), dma((n_g,)), dma((n_g,)),
            dma((n_z,)), dma((n_z,)), dma((n_g,)), dma((n_g,)),
            dma((n_z,)), dma((n_z,)), dma((n_g,)), dma((n_g,)),
            dma((n_g,)), dma((n_g,)), dma((n_z,)), dma((n_z,)),
        ],
        compiler_params=pltpu.CompilerParams(
            collective_id=0, has_side_effects=True, vmem_limit_bytes=48 * 1024 * 1024),
    )(query, passage, positive)
    return loss[0, 0], gq, gp


def solution(mesh):
    return jax.shard_map(
        functools.partial(local, mesh.shape["row"], mesh.shape["col"]),
        mesh=mesh,
        in_specs=(P(("row", "col"), None), P(("row", "col"), None), P(("row", "col"), None)),
        out_specs=(P(), P(("row", "col"), None), P(("row", "col"), None)),
        check_vma=False,
    )
```

```python
import functools

import jax
import jax.numpy as jnp
from jax import lax
from jax.experimental import pallas as pl
from jax.experimental.pallas import tpu as pltpu
from jax.sharding import PartitionSpec as P

logit_scale = 20.0
MESH = pl.DeviceIdType.MESH
F32 = jnp.float32
BF16 = jnp.bfloat16
NT = (((1,), (1,)), ((), ()))
TN = (((0,), (0,)), ((), ()))


def kernel(
    n_row, n_col, q_ref, p_ref, pos_ref, loss_ref, gq_ref, gp_ref,
    q_all, p_all, pos_v, pos_sum, pair_p, pair_q, row_stat, col_stat,
    dq_send, dp_send, dq_recv, dp_recv, loss_r, loss_z,
    local_sem, q_ss, q_rs, p_ss, p_rs, qf_ss, qf_rs, pf_ss, pf_rs, pos_ss, pos_rs,
    rst_ss, rst_rs, cst_ss, cst_rs,
    dq_ss, dq_rs, dp_ss, dp_rs, lr_ss, lr_rs, lz_ss, lz_rs,
):
    rows, width = q_ref.shape
    n_z = n_col // 2
    half_q = n_z * rows
    half_p = n_row * rows
    r = lax.axis_index("row")
    c = lax.axis_index("col")
    z = c // 2
    core = c % 2

    def z_at(d):
        return lax.rem(z + d, n_z)

    def r_at(d):
        return lax.rem(r + d, n_row)

    def z_dev(d):
        return (r, z_at(d) * 2 + core)

    def r_dev(d):
        return (r_at(d), c)

    sibling = (r, z * 2 + 1 - core)

    def copy(device, src, dst, ss, rs, i):
        return pltpu.make_async_remote_copy(
            src_ref=src, dst_ref=dst, send_sem=ss.at[i], recv_sem=rs.at[i],
            device_id=device, device_id_type=MESH)

    z_range = range(1, n_z)
    r_range = range(1, n_row)

    own_p = pltpu.make_async_copy(p_ref, p_all.at[0, r], local_sem.at[0])
    own_q = pltpu.make_async_copy(q_ref, q_all.at[0, z], local_sem.at[1])
    own_pos = pltpu.make_async_copy(pos_ref, pos_v, local_sem.at[2])
    own_p.start()
    own_q.start()
    own_pos.start()

    barrier = pltpu.get_barrier_semaphore()
    for device in [z_dev(d) for d in z_range] + [r_dev(d) for d in r_range] + [sibling]:
        pl.semaphore_signal(barrier, inc=1, device_id=device, device_id_type=MESH)
    pl.semaphore_wait(barrier, n_z + n_row - 1)

    q_copies = [copy(z_dev(d), q_ref, q_all.at[0, z], q_ss, q_rs, d) for d in z_range]
    p_copies = [copy(r_dev(d), p_ref, p_all.at[0, r], p_ss, p_rs, d) for d in r_range]
    q_shared = [copy(sibling, q_ref, q_all.at[1, z], qf_ss, qf_rs, 0)]
    p_shared = [copy(sibling, p_ref, p_all.at[1, r], pf_ss, pf_rs, 0)]
    for cp in q_copies + p_copies + q_shared + p_shared:
        cp.start()

    own_p.wait()
    own_q.wait()
    own_pos.wait()
    q_own = q_all[0, z]
    p_own = p_all[0, r]
    slot = lax.broadcasted_iota(jnp.int32, (rows, rows), 0)
    onehot_t = jnp.where(slot == pos_v[...], 1.0, 0.0).astype(F32)
    paired_p = jnp.dot(onehot_t.T.astype(BF16), p_own, preferred_element_type=F32)
    pair_p[...] = paired_p
    pair_q[...] = jnp.dot(onehot_t.astype(BF16), q_own, preferred_element_type=F32)
    own_sum = logit_scale * jnp.sum(q_own.astype(F32) * paired_p, axis=(0, 1), keepdims=True)
    pos_sum[0] = jnp.broadcast_to(own_sum, (8, 128))
    pos_copy = copy(sibling, pos_sum.at[0], pos_sum.at[1], pos_ss, pos_rs, 0)
    pos_copy.start()

    for d in r_range:
        p_copies[d - 1].wait_recv()
        at = r_at(n_row - d)
        cp = copy(sibling, p_all.at[0, at], p_all.at[1, at], pf_ss, pf_rs, d)
        cp.start()
        p_shared.append(cp)
    for d in z_range:
        q_copies[d - 1].wait_recv()
        at = z_at(n_z - d)
        cp = copy(sibling, q_all.at[0, at], q_all.at[1, at], qf_ss, qf_rs, d)
        cp.start()
        q_shared.append(cp)
    for cp in p_shared + q_shared:
        cp.wait_recv()
    pos_copy.wait()

    q_mat = q_all[...].reshape(2 * half_q, width)
    p_mat = p_all[...].reshape(2 * half_p, width)
    s = logit_scale * lax.dot_general(q_mat, p_mat, NT, preferred_element_type=F32)
    s_t = logit_scale * lax.dot_general(p_mat, q_mat, NT, preferred_element_type=F32)

    def down(x, half):
        return (jnp.sum(x[:half], axis=0, keepdims=True)
                + jnp.sum(x[half:], axis=0, keepdims=True))

    def across(x, half):
        return (jnp.sum(x[:, :half], axis=1, keepdims=True)
                + jnp.sum(x[:, half:], axis=1, keepdims=True))

    col_peak = jnp.max(s, axis=0, keepdims=True)
    col_stat[r, 0:1, :] = col_peak
    col_stat[r, 1:2, :] = down(jnp.exp(s - col_peak), half_q)
    cst = [copy(r_dev(d), col_stat.at[r], col_stat.at[r], cst_ss, cst_rs, d) for d in r_range]
    for cp in cst:
        cp.start()
    row_peak = jnp.max(s_t, axis=0, keepdims=True)
    row_stat[z, 0:1, :] = row_peak
    row_stat[z, 1:2, :] = down(jnp.exp(s_t - row_peak), half_p)
    row_stat[z, 2:3, :] = jnp.broadcast_to(pos_sum[0, 0:1, 0:1] + pos_sum[1, 0:1, 0:1], (1, 2 * half_q))
    rst = [copy(z_dev(d), row_stat.at[z], row_stat.at[z], rst_ss, rst_rs, d) for d in z_range]
    for cp in rst:
        cp.start()
    for cp in cst + rst:
        cp.wait()

    def merge(ref):
        peak = ref[:, 0, :]
        total = ref[:, 1, :]
        top = jnp.max(peak, axis=0, keepdims=True)
        return top + jnp.log(jnp.sum(total * jnp.exp(peak - top), axis=0, keepdims=True))

    row_lse = merge(row_stat)
    col_lse = merge(col_stat)
    row_mat = jnp.broadcast_to(row_lse, (128, 2 * half_q)).T
    row_mat = jnp.concatenate([row_mat] * (2 * half_p // 128), axis=1)
    w = (0.5 * (jnp.exp(s - row_mat) + jnp.exp(s - col_lse))).astype(BF16)

    dq = jnp.dot(w[:half_q], p_mat, preferred_element_type=F32).astype(BF16)
    dq_send[...] = dq.reshape(n_z, rows, width)
    dqc = [copy(z_dev(d), dq_send.at[z_at(d)], dq_recv.at[z], dq_ss, dq_rs, d) for d in z_range]
    for cp in dqc:
        cp.start()
    dp = lax.dot_general(w[:, :half_p], q_mat, TN, preferred_element_type=F32).astype(BF16)
    dp_send[...] = dp.reshape(n_row, rows, width)
    dpc = [copy(r_dev(d), dp_send.at[r_at(d)], dp_recv.at[r], dp_ss, dp_rs, d) for d in r_range]
    for cp in dpc:
        cp.start()
    pos_row = jnp.sum(row_stat[:, 2, 0:1], axis=0, keepdims=True)
    loss_r[r] = jnp.broadcast_to(across(row_lse, half_q) - 2.0 * pos_row, (8, 128))
    loss_z[z] = jnp.broadcast_to(across(col_lse, half_p), (8, 128))
    lrc = [copy(r_dev(d), loss_r.at[r], loss_r.at[r], lr_ss, lr_rs, d) for d in r_range]
    lzc = [copy(z_dev(d), loss_z.at[z], loss_z.at[z], lz_ss, lz_rs, d) for d in z_range]
    for cp in lrc + lzc:
        cp.start()
    dq_recv[z] = dq_send[z]
    dp_recv[r] = dp_send[r]
    for cp in q_copies + p_copies + q_shared + p_shared:
        cp.wait_send()

    for cp in dpc:
        cp.wait()
    acc = dp_recv[0].astype(F32)
    for i in r_range:
        acc += dp_recv[i].astype(F32)
    gp_ref[...] = (logit_scale * (acc - pair_q[...])).astype(BF16)

    for cp in lrc + lzc:
        cp.wait()
    total = jnp.sum(loss_r[:, 0, 0:1], axis=0, keepdims=True) + jnp.sum(loss_z[:, 0, 0:1], axis=0, keepdims=True)
    loss_ref[...] = total / (2.0 * rows * n_row * n_col)

    for cp in dqc:
        cp.wait()
    acc = dq_recv[0].astype(F32)
    for i in z_range:
        acc += dq_recv[i].astype(F32)
    gq_ref[...] = (logit_scale * (acc - pair_p[...])).astype(BF16)


def local(n_row, n_col, query, passage, positive):
    rows, width = query.shape
    n_z = n_col // 2
    dma = pltpu.SemaphoreType.DMA
    loss, gq, gp = pl.pallas_call(
        functools.partial(kernel, n_row, n_col),
        out_shape=(
            jax.ShapeDtypeStruct((1, 1), F32),
            jax.ShapeDtypeStruct((rows, width), BF16),
            jax.ShapeDtypeStruct((rows, width), BF16),
        ),
        in_specs=[pl.BlockSpec(memory_space=pltpu.HBM)] * 3,
        out_specs=[pl.BlockSpec(memory_space=pltpu.VMEM)] * 3,
        scratch_shapes=[
            pltpu.VMEM((2, n_z, rows, width), BF16),
            pltpu.VMEM((2, n_row, rows, width), BF16),
            pltpu.VMEM((1, rows), jnp.int32),
            pltpu.VMEM((2, 8, 128), F32),
            pltpu.VMEM((rows, width), F32),
            pltpu.VMEM((rows, width), F32),
            pltpu.VMEM((n_z, 8, 2 * n_z * rows), F32),
            pltpu.VMEM((n_row, 8, 2 * n_row * rows), F32),
            pltpu.VMEM((n_z, rows, width), BF16),
            pltpu.VMEM((n_row, rows, width), BF16),
            pltpu.VMEM((n_z, rows, width), BF16),
            pltpu.VMEM((n_row, rows, width), BF16),
            pltpu.VMEM((n_row, 8, 128), F32),
            pltpu.VMEM((n_z, 8, 128), F32),
            dma((3,)),
            dma((n_z,)), dma((n_z,)), dma((n_row,)), dma((n_row,)),
            dma((n_z,)), dma((n_z,)), dma((n_row,)), dma((n_row,)),
            dma((1,)), dma((1,)),
            dma((n_z,)), dma((n_z,)), dma((n_row,)), dma((n_row,)),
            dma((n_z,)), dma((n_z,)), dma((n_row,)), dma((n_row,)),
            dma((n_row,)), dma((n_row,)), dma((n_z,)), dma((n_z,)),
        ],
        compiler_params=pltpu.CompilerParams(
            collective_id=0, has_side_effects=True, vmem_limit_bytes=48 * 1024 * 1024),
    )(query, passage, positive)
    return loss[0, 0], gq, gp


def solution(mesh):
    return jax.shard_map(
        functools.partial(local, mesh.shape["row"], mesh.shape["col"]),
        mesh=mesh,
        in_specs=(P(("row", "col"), None), P(("row", "col"), None), P(("row", "col"), None)),
        out_specs=(P(), P(("row", "col"), None), P(("row", "col"), None)),
        check_vma=False,
    )
```

```python
import functools

import jax
import jax.numpy as jnp
from jax import lax
from jax.experimental import pallas as pl
from jax.experimental.pallas import tpu as pltpu
from jax.sharding import PartitionSpec as P

logit_scale = 20.0
MESH = pl.DeviceIdType.MESH
F32 = jnp.float32
BF16 = jnp.bfloat16
NT = (((1,), (1,)), ((), ()))
TN = (((0,), (0,)), ((), ()))


def kernel(
    n_row, n_col, q_ref, p_ref, pos_ref, loss_ref, gq_ref, gp_ref,
    q_all, p_all, pos_v, pos_sum, pair_p, pair_q, row_stat, col_stat,
    dq_send, dp_send, dq_recv, dp_recv, loss_r, loss_z,
    local_sem, q_ss, q_rs, p_ss, p_rs, qf_ss, qf_rs, pf_ss, pf_rs, pos_ss, pos_rs,
    rst_ss, rst_rs, cst_ss, cst_rs,
    dq_ss, dq_rs, dp_ss, dp_rs, lr_ss, lr_rs, lz_ss, lz_rs,
):
    rows, width = q_ref.shape
    n_z = n_col // 2
    half_q = n_z * rows
    half_p = n_row * rows
    r = lax.axis_index("row")
    c = lax.axis_index("col")
    z = c // 2
    core = c % 2

    def z_at(d):
        return lax.rem(z + d, n_z)

    def r_at(d):
        return lax.rem(r + d, n_row)

    def z_dev(d):
        return (r, z_at(d) * 2 + core)

    def r_dev(d):
        return (r_at(d), c)

    sibling = (r, z * 2 + 1 - core)

    def copy(device, src, dst, ss, rs, i):
        return pltpu.make_async_remote_copy(
            src_ref=src, dst_ref=dst, send_sem=ss.at[i], recv_sem=rs.at[i],
            device_id=device, device_id_type=MESH)

    z_range = range(1, n_z)
    r_range = range(1, n_row)

    own_p = pltpu.make_async_copy(p_ref, p_all.at[0, r], local_sem.at[0])
    own_q = pltpu.make_async_copy(q_ref, q_all.at[0, z], local_sem.at[1])
    own_pos = pltpu.make_async_copy(pos_ref, pos_v, local_sem.at[2])
    own_p.start()
    own_q.start()
    own_pos.start()

    barrier = pltpu.get_barrier_semaphore()
    for device in [z_dev(d) for d in z_range] + [r_dev(d) for d in r_range] + [sibling]:
        pl.semaphore_signal(barrier, inc=1, device_id=device, device_id_type=MESH)
    pl.semaphore_wait(barrier, n_z + n_row - 1)

    q_copies = [copy(z_dev(d), q_ref, q_all.at[0, z], q_ss, q_rs, d) for d in z_range]
    p_copies = [copy(r_dev(d), p_ref, p_all.at[0, r], p_ss, p_rs, d) for d in r_range]
    q_shared = [copy(sibling, q_ref, q_all.at[1, z], qf_ss, qf_rs, 0)]
    p_shared = [copy(sibling, p_ref, p_all.at[1, r], pf_ss, pf_rs, 0)]
    for cp in q_copies + p_copies + q_shared + p_shared:
        cp.start()

    own_p.wait()
    own_q.wait()
    own_pos.wait()
    q_own = q_all[0, z]
    p_own = p_all[0, r]
    slot = lax.broadcasted_iota(jnp.int32, (rows, rows), 0)
    onehot_t = jnp.where(slot == pos_v[...], 1.0, 0.0).astype(F32)
    paired_p = jnp.dot(onehot_t.T.astype(BF16), p_own, preferred_element_type=F32)
    pair_p[...] = paired_p
    pair_q[...] = jnp.dot(onehot_t.astype(BF16), q_own, preferred_element_type=F32)
    own_sum = logit_scale * jnp.sum(q_own.astype(F32) * paired_p, axis=(0, 1), keepdims=True)
    pos_sum[0] = jnp.broadcast_to(own_sum, (8, 128))
    pos_copy = copy(sibling, pos_sum.at[0], pos_sum.at[1], pos_ss, pos_rs, 0)
    pos_copy.start()

    for d in r_range:
        p_copies[d - 1].wait_recv()
        at = r_at(n_row - d)
        cp = copy(sibling, p_all.at[0, at], p_all.at[1, at], pf_ss, pf_rs, d)
        cp.start()
        p_shared.append(cp)
    for d in z_range:
        q_copies[d - 1].wait_recv()
        at = z_at(n_z - d)
        cp = copy(sibling, q_all.at[0, at], q_all.at[1, at], qf_ss, qf_rs, d)
        cp.start()
        q_shared.append(cp)
    for cp in p_shared + q_shared:
        cp.wait_recv()
    pos_copy.wait()

    q_mat = q_all[...].reshape(2 * half_q, width)
    p_mat = p_all[...].reshape(2 * half_p, width)
    s = logit_scale * lax.dot_general(q_mat, p_mat, NT, preferred_element_type=F32)
    s_t = logit_scale * lax.dot_general(p_mat, q_mat, NT, preferred_element_type=F32)

    def down(x, half):
        return (jnp.sum(x[:half], axis=0, keepdims=True)
                + jnp.sum(x[half:], axis=0, keepdims=True))

    def across(x, half):
        return (jnp.sum(x[:, :half], axis=1, keepdims=True)
                + jnp.sum(x[:, half:], axis=1, keepdims=True))

    col_peak = jnp.max(s, axis=0, keepdims=True)
    col_stat[r, 0:1, :] = col_peak
    col_stat[r, 1:2, :] = down(jnp.exp(s - col_peak), half_q)
    cst = [copy(r_dev(d), col_stat.at[r], col_stat.at[r], cst_ss, cst_rs, d) for d in r_range]
    for cp in cst:
        cp.start()
    row_peak = jnp.max(s_t, axis=0, keepdims=True)
    row_stat[z, 0:1, :] = row_peak
    row_stat[z, 1:2, :] = down(jnp.exp(s_t - row_peak), half_p)
    row_stat[z, 2:3, :] = jnp.broadcast_to(pos_sum[0, 0:1, 0:1] + pos_sum[1, 0:1, 0:1], (1, 2 * half_q))
    rst = [copy(z_dev(d), row_stat.at[z], row_stat.at[z], rst_ss, rst_rs, d) for d in z_range]
    for cp in rst:
        cp.start()
    for cp in cst + rst:
        cp.wait()

    def merge(ref):
        peak = ref[:, 0, :]
        total = ref[:, 1, :]
        top = jnp.max(peak, axis=0, keepdims=True)
        return top + jnp.log(jnp.sum(total * jnp.exp(peak - top), axis=0, keepdims=True))

    row_lse = merge(row_stat)
    col_lse = merge(col_stat)
    row_mat = jnp.broadcast_to(row_lse, (128, 2 * half_q)).T
    row_mat = jnp.concatenate([row_mat] * (2 * half_p // 128), axis=1)
    w = (0.5 * (jnp.exp(s - row_mat) + jnp.exp(s - col_lse))).astype(BF16)

    dq = jnp.dot(w[:half_q], p_mat, preferred_element_type=F32).astype(BF16)
    dq_send[...] = dq.reshape(n_z, rows, width)
    dqc = [copy(z_dev(d), dq_send.at[z_at(d)], dq_recv.at[z], dq_ss, dq_rs, d) for d in z_range]
    for cp in dqc:
        cp.start()
    dp = lax.dot_general(w[:, :half_p], q_mat, TN, preferred_element_type=F32).astype(BF16)
    dp_send[...] = dp.reshape(n_row, rows, width)
    dpc = [copy(r_dev(d), dp_send.at[r_at(d)], dp_recv.at[r], dp_ss, dp_rs, d) for d in r_range]
    for cp in dpc:
        cp.start()
    pos_row = jnp.sum(row_stat[:, 2, 0:1], axis=0, keepdims=True)
    loss_r[r] = jnp.broadcast_to(across(row_lse, half_q) - 2.0 * pos_row, (8, 128))
    loss_z[z] = jnp.broadcast_to(across(col_lse, half_p), (8, 128))
    lrc = [copy(r_dev(d), loss_r.at[r], loss_r.at[r], lr_ss, lr_rs, d) for d in r_range]
    lzc = [copy(z_dev(d), loss_z.at[z], loss_z.at[z], lz_ss, lz_rs, d) for d in z_range]
    for cp in lrc + lzc:
        cp.start()
    dq_recv[z] = dq_send[z]
    dp_recv[r] = dp_send[r]
    for cp in q_copies + p_copies + q_shared + p_shared:
        cp.wait_send()

    for cp in dpc:
        cp.wait()
    acc = dp_recv[0].astype(F32)
    for i in r_range:
        acc += dp_recv[i].astype(F32)
    gp_ref[...] = (logit_scale * (acc - pair_q[...])).astype(BF16)

    for cp in lrc + lzc:
        cp.wait()
    total = jnp.sum(loss_r[:, 0, 0:1], axis=0, keepdims=True) + jnp.sum(loss_z[:, 0, 0:1], axis=0, keepdims=True)
    loss_ref[...] = total / (2.0 * rows * n_row * n_col)

    for cp in dqc:
        cp.wait()
    acc = dq_recv[0].astype(F32)
    for i in z_range:
        acc += dq_recv[i].astype(F32)
    gq_ref[...] = (logit_scale * (acc - pair_p[...])).astype(BF16)


def local(n_row, n_col, query, passage, positive):
    rows, width = query.shape
    n_z = n_col // 2
    dma = pltpu.SemaphoreType.DMA
    loss, gq, gp = pl.pallas_call(
        functools.partial(kernel, n_row, n_col),
        out_shape=(
            jax.ShapeDtypeStruct((1, 1), F32),
            jax.ShapeDtypeStruct((rows, width), BF16),
            jax.ShapeDtypeStruct((rows, width), BF16),
        ),
        in_specs=[pl.BlockSpec(memory_space=pltpu.HBM)] * 3,
        out_specs=[pl.BlockSpec(memory_space=pltpu.VMEM)] * 3,
        scratch_shapes=[
            pltpu.VMEM((2, n_z, rows, width), BF16),
            pltpu.VMEM((2, n_row, rows, width), BF16),
            pltpu.VMEM((1, rows), jnp.int32),
            pltpu.VMEM((2, 8, 128), F32),
            pltpu.VMEM((rows, width), F32),
            pltpu.VMEM((rows, width), F32),
            pltpu.VMEM((n_z, 8, 2 * n_z * rows), F32),
            pltpu.VMEM((n_row, 8, 2 * n_row * rows), F32),
            pltpu.VMEM((n_z, rows, width), BF16),
            pltpu.VMEM((n_row, rows, width), BF16),
            pltpu.VMEM((n_z, rows, width), BF16),
            pltpu.VMEM((n_row, rows, width), BF16),
            pltpu.VMEM((n_row, 8, 128), F32),
            pltpu.VMEM((n_z, 8, 128), F32),
            dma((3,)),
            dma((n_z,)), dma((n_z,)), dma((n_row,)), dma((n_row,)),
            dma((n_z,)), dma((n_z,)), dma((n_row,)), dma((n_row,)),
            dma((1,)), dma((1,)),
            dma((n_z,)), dma((n_z,)), dma((n_row,)), dma((n_row,)),
            dma((n_z,)), dma((n_z,)), dma((n_row,)), dma((n_row,)),
            dma((n_row,)), dma((n_row,)), dma((n_z,)), dma((n_z,)),
        ],
        compiler_params=pltpu.CompilerParams(
            collective_id=0, has_side_effects=True, vmem_limit_bytes=48 * 1024 * 1024),
    )(*(pltpu.with_memory_space_constraint(x, pltpu.HBM) for x in (query, passage, positive)))
    return loss[0, 0], gq, gp


def solution(mesh):
    return jax.shard_map(
        functools.partial(local, mesh.shape["row"], mesh.shape["col"]),
        mesh=mesh,
        in_specs=(P(("row", "col"), None), P(("row", "col"), None), P(("row", "col"), None)),
        out_specs=(P(), P(("row", "col"), None), P(("row", "col"), None)),
        check_vma=False,
    )
```

```python
import functools

import jax
import jax.numpy as jnp
from jax import lax
from jax.experimental import pallas as pl
from jax.experimental.pallas import tpu as pltpu
from jax.sharding import PartitionSpec as P

logit_scale = 20.0
MESH = pl.DeviceIdType.MESH
F32 = jnp.float32
BF16 = jnp.bfloat16
NT = (((1,), (1,)), ((), ()))
TN = (((0,), (0,)), ((), ()))


def kernel(
    n_row, n_col, q_ref, p_ref, pos_ref, loss_ref, gq_ref, gp_ref,
    q_all, p_all, pos_v, pos_sum, pair_p, pair_q, row_stat, col_stat,
    dq_send, dp_send, dq_recv, dp_recv, loss_r, loss_z,
    local_sem, q_ss, q_rs, p_ss, p_rs, qf_ss, qf_rs, pf_ss, pf_rs, pos_ss, pos_rs,
    rst_ss, rst_rs, cst_ss, cst_rs,
    dq_ss, dq_rs, dp_ss, dp_rs, lr_ss, lr_rs, lz_ss, lz_rs,
):
    rows, width = q_ref.shape
    n_z = n_col // 2
    half_q = n_z * rows
    half_p = n_row * rows
    r = lax.axis_index("row")
    c = lax.axis_index("col")
    z = c // 2
    core = c % 2

    def z_at(d):
        return lax.rem(z + d, n_z)

    def r_at(d):
        return lax.rem(r + d, n_row)

    def z_dev(d):
        return (r, z_at(d) * 2 + core)

    def r_dev(d):
        return (r_at(d), c)

    sibling = (r, z * 2 + 1 - core)

    def copy(device, src, dst, ss, rs, i):
        return pltpu.make_async_remote_copy(
            src_ref=src, dst_ref=dst, send_sem=ss.at[i], recv_sem=rs.at[i],
            device_id=device, device_id_type=MESH)

    z_range = range(1, n_z)
    r_range = range(1, n_row)

    own_p = pltpu.make_async_copy(p_ref, p_all.at[0, r], local_sem.at[0])
    own_q = pltpu.make_async_copy(q_ref, q_all.at[0, z], local_sem.at[1])
    own_pos = pltpu.make_async_copy(pos_ref, pos_v, local_sem.at[2])
    own_p.start()
    own_q.start()
    own_pos.start()

    barrier = pltpu.get_barrier_semaphore()
    for device in [z_dev(d) for d in z_range] + [r_dev(d) for d in r_range] + [sibling]:
        pl.semaphore_signal(barrier, inc=1, device_id=device, device_id_type=MESH)
    pl.semaphore_wait(barrier, n_z + n_row - 1)

    q_copies = [copy(z_dev(d), q_ref, q_all.at[0, z], q_ss, q_rs, d) for d in z_range]
    p_copies = [copy(r_dev(d), p_ref, p_all.at[0, r], p_ss, p_rs, d) for d in r_range]
    q_shared = [copy(sibling, q_ref, q_all.at[1, z], qf_ss, qf_rs, 0)]
    p_shared = [copy(sibling, p_ref, p_all.at[1, r], pf_ss, pf_rs, 0)]
    for cp in q_copies + p_copies + q_shared + p_shared:
        cp.start()

    own_p.wait()
    own_q.wait()
    own_pos.wait()
    q_own = q_all[0, z]
    p_own = p_all[0, r]
    slot = lax.broadcasted_iota(jnp.int32, (rows, rows), 0)
    onehot_t = jnp.where(slot == pos_v[...], 1.0, 0.0).astype(F32)
    paired_p = jnp.dot(onehot_t.T.astype(BF16), p_own, preferred_element_type=F32)
    pair_p[...] = paired_p
    pair_q[...] = jnp.dot(onehot_t.astype(BF16), q_own, preferred_element_type=F32)
    own_sum = logit_scale * jnp.sum(q_own.astype(F32) * paired_p, axis=(0, 1), keepdims=True)
    pos_sum[0] = jnp.broadcast_to(own_sum, (8, 128))
    pos_copy = copy(sibling, pos_sum.at[0], pos_sum.at[1], pos_ss, pos_rs, 0)
    pos_copy.start()

    for d in r_range:
        p_copies[d - 1].wait_recv()
        at = r_at(n_row - d)
        cp = copy(sibling, p_all.at[0, at], p_all.at[1, at], pf_ss, pf_rs, d)
        cp.start()
        p_shared.append(cp)
    for d in z_range:
        q_copies[d - 1].wait_recv()
        at = z_at(n_z - d)
        cp = copy(sibling, q_all.at[0, at], q_all.at[1, at], qf_ss, qf_rs, d)
        cp.start()
        q_shared.append(cp)
    for cp in p_shared + q_shared:
        cp.wait_recv()
    pos_copy.wait()

    q_mat = q_all[...].reshape(2 * half_q, width)
    p_mat = p_all[...].reshape(2 * half_p, width)
    s = logit_scale * lax.dot_general(q_mat, p_mat, NT, preferred_element_type=F32)
    s_t = logit_scale * lax.dot_general(p_mat, q_mat, NT, preferred_element_type=F32)

    def down(x, half):
        return (jnp.sum(x[:half], axis=0, keepdims=True)
                + jnp.sum(x[half:], axis=0, keepdims=True))

    def across(x, half):
        return (jnp.sum(x[:, :half], axis=1, keepdims=True)
                + jnp.sum(x[:, half:], axis=1, keepdims=True))

    col_peak = jnp.max(s, axis=0, keepdims=True)
    col_stat[r, 0:1, :] = col_peak
    col_stat[r, 1:2, :] = down(jnp.exp(s - col_peak), half_q)
    cst = [copy(r_dev(d), col_stat.at[r], col_stat.at[r], cst_ss, cst_rs, d) for d in r_range]
    for cp in cst:
        cp.start()
    row_peak = jnp.max(s_t, axis=0, keepdims=True)
    row_stat[z, 0:1, :] = row_peak
    row_stat[z, 1:2, :] = down(jnp.exp(s_t - row_peak), half_p)
    row_stat[z, 2:3, :] = jnp.broadcast_to(pos_sum[0, 0:1, 0:1] + pos_sum[1, 0:1, 0:1], (1, 2 * half_q))
    rst = [copy(z_dev(d), row_stat.at[z], row_stat.at[z], rst_ss, rst_rs, d) for d in z_range]
    for cp in rst:
        cp.start()
    for cp in cst + rst:
        cp.wait()

    def merge(ref):
        peak = ref[:, 0, :]
        total = ref[:, 1, :]
        top = jnp.max(peak, axis=0, keepdims=True)
        return top + jnp.log(jnp.sum(total * jnp.exp(peak - top), axis=0, keepdims=True))

    row_lse = merge(row_stat)
    col_lse = merge(col_stat)
    row_mat = jnp.broadcast_to(row_lse, (128, 2 * half_q)).T
    row_mat = jnp.concatenate([row_mat] * (2 * half_p // 128), axis=1)
    w = (0.5 * (jnp.exp(s - row_mat) + jnp.exp(s - col_lse))).astype(BF16)

    dq = jnp.dot(w[:half_q], p_mat, preferred_element_type=F32).astype(BF16)
    dq_send[...] = dq.reshape(n_z, rows, width)
    dqc = [copy(z_dev(d), dq_send.at[z_at(d)], dq_recv.at[z], dq_ss, dq_rs, d) for d in z_range]
    for cp in dqc:
        cp.start()
    dp = lax.dot_general(w[:, :half_p], q_mat, TN, preferred_element_type=F32).astype(BF16)
    dp_send[...] = dp.reshape(n_row, rows, width)
    dpc = [copy(r_dev(d), dp_send.at[r_at(d)], dp_recv.at[r], dp_ss, dp_rs, d) for d in r_range]
    for cp in dpc:
        cp.start()
    pos_row = jnp.sum(row_stat[:, 2, 0:1], axis=0, keepdims=True)
    loss_r[r] = jnp.broadcast_to(across(row_lse, half_q) - 2.0 * pos_row, (8, 128))
    loss_z[z] = jnp.broadcast_to(across(col_lse, half_p), (8, 128))
    lrc = [copy(r_dev(d), loss_r.at[r], loss_r.at[r], lr_ss, lr_rs, d) for d in r_range]
    lzc = [copy(z_dev(d), loss_z.at[z], loss_z.at[z], lz_ss, lz_rs, d) for d in z_range]
    for cp in lrc + lzc:
        cp.start()
    dq_recv[z] = dq_send[z]
    dp_recv[r] = dp_send[r]
    for cp in q_copies + p_copies + q_shared + p_shared:
        cp.wait_send()

    for cp in dpc:
        cp.wait()
    acc = dp_recv[0].astype(F32)
    for i in r_range:
        acc += dp_recv[i].astype(F32)
    gp_ref[...] = (logit_scale * (acc - pair_q[...])).astype(BF16)

    for cp in lrc + lzc:
        cp.wait()
    total = jnp.sum(loss_r[:, 0, 0:1], axis=0, keepdims=True) + jnp.sum(loss_z[:, 0, 0:1], axis=0, keepdims=True)
    loss_ref[...] = jnp.broadcast_to(total / (2.0 * rows * n_row * n_col), (8, 128))

    for cp in dqc:
        cp.wait()
    acc = dq_recv[0].astype(F32)
    for i in z_range:
        acc += dq_recv[i].astype(F32)
    gq_ref[...] = (logit_scale * (acc - pair_p[...])).astype(BF16)


def hand_out(loss_ref, gq_ref, gp_ref, loss_out, gq_out, gp_out, loss_v, sem):
    loss_v[...] = loss_ref[0:1, 0:1]
    pairs = ((gq_ref, gq_out), (gp_ref, gp_out), (loss_v, loss_out))
    copies = [pltpu.make_async_copy(src, dst, sem.at[i]) for i, (src, dst) in enumerate(pairs)]
    for cp in copies:
        cp.start()
    for cp in copies:
        cp.wait()


def local(n_row, n_col, query, passage, positive):
    rows, width = query.shape
    n_z = n_col // 2
    dma = pltpu.SemaphoreType.DMA
    loss, gq, gp = pl.pallas_call(
        functools.partial(kernel, n_row, n_col),
        out_shape=(
            jax.ShapeDtypeStruct((8, 128), F32),
            jax.ShapeDtypeStruct((rows, width), BF16),
            jax.ShapeDtypeStruct((rows, width), BF16),
        ),
        in_specs=[pl.BlockSpec(memory_space=pltpu.HBM)] * 3,
        out_specs=[pl.BlockSpec(memory_space=pltpu.VMEM)] * 3,
        scratch_shapes=[
            pltpu.VMEM((2, n_z, rows, width), BF16),
            pltpu.VMEM((2, n_row, rows, width), BF16),
            pltpu.VMEM((1, rows), jnp.int32),
            pltpu.VMEM((2, 8, 128), F32),
            pltpu.VMEM((rows, width), F32),
            pltpu.VMEM((rows, width), F32),
            pltpu.VMEM((n_z, 8, 2 * n_z * rows), F32),
            pltpu.VMEM((n_row, 8, 2 * n_row * rows), F32),
            pltpu.VMEM((n_z, rows, width), BF16),
            pltpu.VMEM((n_row, rows, width), BF16),
            pltpu.VMEM((n_z, rows, width), BF16),
            pltpu.VMEM((n_row, rows, width), BF16),
            pltpu.VMEM((n_row, 8, 128), F32),
            pltpu.VMEM((n_z, 8, 128), F32),
            dma((3,)),
            dma((n_z,)), dma((n_z,)), dma((n_row,)), dma((n_row,)),
            dma((n_z,)), dma((n_z,)), dma((n_row,)), dma((n_row,)),
            dma((1,)), dma((1,)),
            dma((n_z,)), dma((n_z,)), dma((n_row,)), dma((n_row,)),
            dma((n_z,)), dma((n_z,)), dma((n_row,)), dma((n_row,)),
            dma((n_row,)), dma((n_row,)), dma((n_z,)), dma((n_z,)),
        ],
        compiler_params=pltpu.CompilerParams(
            collective_id=0, has_side_effects=True, vmem_limit_bytes=48 * 1024 * 1024),
    )(*(pltpu.with_memory_space_constraint(x, pltpu.HBM) for x in (query, passage, positive)))
    loss, gq, gp = pl.pallas_call(
        hand_out,
        out_shape=(
            jax.ShapeDtypeStruct((1, 1), F32),
            jax.ShapeDtypeStruct(gq.shape, BF16),
            jax.ShapeDtypeStruct(gp.shape, BF16),
        ),
        in_specs=[pl.BlockSpec(memory_space=pltpu.VMEM)] * 3,
        out_specs=[pl.BlockSpec(memory_space=pl.ANY)] * 3,
        scratch_shapes=[pltpu.VMEM((1, 1), F32), dma((3,))],
    )(loss, gq, gp)
    return loss[0, 0], gq, gp


def solution(mesh):
    return jax.shard_map(
        functools.partial(local, mesh.shape["row"], mesh.shape["col"]),
        mesh=mesh,
        in_specs=(P(("row", "col"), None), P(("row", "col"), None), P(("row", "col"), None)),
        out_specs=(P(), P(("row", "col"), None), P(("row", "col"), None)),
        check_vma=False,
    )
```

```python
import functools

import jax
import jax.numpy as jnp
from jax import lax
from jax.experimental import pallas as pl
from jax.experimental.pallas import tpu as pltpu
from jax.sharding import PartitionSpec as P

logit_scale = 20.0
MESH = pl.DeviceIdType.MESH
F32 = jnp.float32
BF16 = jnp.bfloat16
NT = (((1,), (1,)), ((), ()))
TN = (((0,), (0,)), ((), ()))


def kernel(
    n_row, n_col, q_ref, p_ref, pos_ref, loss_ref, gq_ref, gp_ref,
    q_all, p_all, pos_v, pos_sum, pair_p, pair_q, row_stat, col_stat,
    dq_send, dp_send, dq_recv, dp_recv, dq_relay, loss_r, loss_z, gq_v, gp_v, loss_v,
    local_sem, q_ss, q_rs, p_ss, p_rs, qf_ss, qf_rs, pf_ss, pf_rs, pos_ss, pos_rs,
    rst_ss, rst_rs, cst_ss, cst_rs,
    dq_ss, dq_rs, dp_ss, dp_rs, lr_ss, lr_rs, lz_ss, lz_rs,
):
    rows, width = q_ref.shape
    n_z = n_col // 2
    half_q = n_z * rows
    half_p = n_row * rows
    r = lax.axis_index("row")
    c = lax.axis_index("col")
    z = c // 2
    core = c % 2

    def z_at(d):
        return lax.rem(z + d, n_z)

    def r_at(d):
        return lax.rem(r + d, n_row)

    def z_dev(d):
        return (r, z_at(d) * 2 + core)

    def r_dev(d):
        return (r_at(d), c)

    sibling = (r, z * 2 + 1 - core)

    def copy(device, src, dst, ss, rs, i):
        return pltpu.make_async_remote_copy(
            src_ref=src, dst_ref=dst, send_sem=ss.at[i], recv_sem=rs.at[i],
            device_id=device, device_id_type=MESH)

    relayed = n_z >= 4
    last = n_z - 1
    z_range = range(1, n_z)
    z_order = list(z_range)
    if relayed:
        inner = [2] + ([n_z - 2] if n_z > 4 else []) + list(range(3, n_z - 2))
        low = z < n_z // 2
        z_order = inner + [jnp.where(low, last, 1), jnp.where(low, 1, last)]

    def crosses(d):
        return ((z == 0) & (d == last)) | ((z == last) & (d == 1))

    def unless_crossing(d, action):
        if relayed and not (isinstance(d, int) and 1 < d < last):
            pl.when(jnp.logical_not(crosses(d)))(action)
        else:
            action()

    r_range = range(1, n_row)

    own_p = pltpu.make_async_copy(p_ref, p_all.at[0, r], local_sem.at[0])
    own_q = pltpu.make_async_copy(q_ref, q_all.at[0, z], local_sem.at[1])
    own_pos = pltpu.make_async_copy(pos_ref, pos_v, local_sem.at[2])
    own_p.start()
    own_q.start()
    own_pos.start()

    barrier = pltpu.get_barrier_semaphore()
    for device in [z_dev(d) for d in z_range] + [r_dev(d) for d in r_range] + [sibling]:
        pl.semaphore_signal(barrier, inc=1, device_id=device, device_id_type=MESH)
    pl.semaphore_wait(barrier, n_z + n_row - 1)

    q_copies = [copy(z_dev(d), q_ref, q_all.at[0, z], q_ss, q_rs, d) for d in z_order]
    p_copies = [copy(r_dev(d), p_ref, p_all.at[0, r], p_ss, p_rs, d) for d in r_range]
    q_shared = [copy(sibling, q_ref, q_all.at[1, z], qf_ss, qf_rs, 0)]
    p_shared = [copy(sibling, p_ref, p_all.at[1, r], pf_ss, pf_rs, 0)]
    for d, cp in zip(z_order, q_copies):
        unless_crossing(d, cp.start)
    for cp in p_copies + q_shared + p_shared:
        cp.start()

    own_p.wait()
    own_q.wait()
    own_pos.wait()
    q_own = q_all[0, z]
    p_own = p_all[0, r]
    slot = lax.broadcasted_iota(jnp.int32, (rows, rows), 0)
    onehot_t = jnp.where(slot == pos_v[...], 1.0, 0.0).astype(F32)
    paired_p = jnp.dot(onehot_t.T.astype(BF16), p_own, preferred_element_type=F32)
    pair_p[...] = paired_p
    pair_q[...] = jnp.dot(onehot_t.astype(BF16), q_own, preferred_element_type=F32)
    own_sum = logit_scale * jnp.sum(q_own.astype(F32) * paired_p, axis=(0, 1), keepdims=True)
    pos_sum[0] = jnp.broadcast_to(own_sum, (8, 128))
    pos_copy = copy(sibling, pos_sum.at[0], pos_sum.at[1], pos_ss, pos_rs, 0)
    pos_copy.start()

    def share_q(i):
        d = z_order[i]
        at = z_at(n_z - d)
        cp = copy(sibling, q_all.at[0, at], q_all.at[1, at], qf_ss, qf_rs, d)
        cp.start()
        q_shared.append(cp)

    first_q = 0
    if relayed:
        to_last = pltpu.make_async_remote_copy(
            src_ref=q_all.at[0, 0], dst_ref=q_all.at[0, 0], send_sem=q_ss.at[0], recv_sem=q_rs.at[last],
            device_id=z_dev(1), device_id_type=MESH)
        to_first = pltpu.make_async_remote_copy(
            src_ref=q_all.at[0, last], dst_ref=q_all.at[0, last], send_sem=q_ss.at[0], recv_sem=q_rs.at[1],
            device_id=z_dev(last), device_id_type=MESH)
        first_q = 1 if n_z == 4 else 2
        for i in range(first_q):
            q_copies[i].wait_recv()
        pl.when(z == n_z - 2)(to_last.start)
        pl.when(z == 1)(to_first.start)
        for i in range(first_q):
            share_q(i)
    for d in r_range:
        p_copies[d - 1].wait_recv()
        at = r_at(n_row - d)
        cp = copy(sibling, p_all.at[0, at], p_all.at[1, at], pf_ss, pf_rs, d)
        cp.start()
        p_shared.append(cp)
    for i in range(first_q, n_z - 1):
        q_copies[i].wait_recv()
        share_q(i)
    for cp in p_shared + q_shared:
        cp.wait_recv()
    pos_copy.wait()

    q_mat = q_all[...].reshape(2 * half_q, width)
    p_mat = p_all[...].reshape(2 * half_p, width)
    s = logit_scale * lax.dot_general(q_mat, p_mat, NT, preferred_element_type=F32)
    s_t = logit_scale * lax.dot_general(p_mat, q_mat, NT, preferred_element_type=F32)

    def down(x, half):
        return (jnp.sum(x[:half], axis=0, keepdims=True)
                + jnp.sum(x[half:], axis=0, keepdims=True))

    def across(x, half):
        return (jnp.sum(x[:, :half], axis=1, keepdims=True)
                + jnp.sum(x[:, half:], axis=1, keepdims=True))

    col_peak = jnp.max(s, axis=0, keepdims=True)
    col_stat[r, 0:1, :] = col_peak
    col_stat[r, 1:2, :] = down(jnp.exp(s - col_peak), half_q)
    cst = [copy(r_dev(d), col_stat.at[r], col_stat.at[r], cst_ss, cst_rs, d) for d in r_range]
    for cp in cst:
        cp.start()
    row_peak = jnp.max(s_t, axis=0, keepdims=True)
    row_stat[z, 0:1, :] = row_peak
    row_stat[z, 1:2, :] = down(jnp.exp(s_t - row_peak), half_p)
    row_stat[z, 2:3, :] = jnp.broadcast_to(pos_sum[0, 0:1, 0:1] + pos_sum[1, 0:1, 0:1], (1, 2 * half_q))
    rst = [copy(z_dev(d), row_stat.at[z], row_stat.at[z], rst_ss, rst_rs, d) for d in z_range]
    for cp in rst:
        cp.start()
    for cp in cst + rst:
        cp.wait()

    def merge(ref):
        peak = ref[:, 0, :]
        total = ref[:, 1, :]
        top = jnp.max(peak, axis=0, keepdims=True)
        return top + jnp.log(jnp.sum(total * jnp.exp(peak - top), axis=0, keepdims=True))

    row_lse = merge(row_stat)
    col_lse = merge(col_stat)
    row_mat = jnp.broadcast_to(row_lse, (128, 2 * half_q)).T
    row_mat = jnp.concatenate([row_mat] * (2 * half_p // 128), axis=1)
    w = (0.5 * (jnp.exp(s - row_mat) + jnp.exp(s - col_lse))).astype(BF16)

    dq = jnp.dot(w[:half_q], p_mat, preferred_element_type=F32).astype(BF16)
    dq_send[...] = dq.reshape(n_z, rows, width)
    dqc = [copy(z_dev(d), dq_send.at[z_at(d)], dq_recv.at[z], dq_ss, dq_rs, d) for d in z_order]
    if relayed:
        up = copy(z_dev(1), dq_send.at[last], dq_relay, dq_ss, dq_rs, 0)
        down_ = copy(z_dev(last), dq_send.at[0], dq_relay, dq_ss, dq_rs, 0)
        pl.when(z == 0)(up.start)
        pl.when(z == last)(down_.start)
        adds = (z == 1) | (z == n_z - 2)
        far = jnp.where(z == 1, last, 0)
    for d, cp in zip(z_order, dqc):
        if relayed:
            target = z_at(d)
            goes_late = adds & (target == far)
            pl.when(jnp.logical_not(crosses(d) | goes_late))(cp.start)
        else:
            cp.start()
    dp = lax.dot_general(w[:, :half_p], q_mat, TN, preferred_element_type=F32).astype(BF16)
    dp_send[...] = dp.reshape(n_row, rows, width)
    dpc = [copy(r_dev(d), dp_send.at[r_at(d)], dp_recv.at[r], dp_ss, dp_rs, d) for d in r_range]
    for cp in dpc:
        cp.start()
    if relayed:
        @pl.when(adds)
        def _():
            up.wait_recv()
            dq_send[far] = (dq_send[far].astype(F32) + dq_relay[...].astype(F32)).astype(BF16)
            copy(z_dev(far - z + n_z), dq_send.at[far], dq_recv.at[z], dq_ss, dq_rs, lax.rem(far - z + n_z, n_z)).start()

        @pl.when((z == 0) | (z == last))
        def _():
            dq_recv[last - z] = jnp.zeros((rows, width), BF16)
    pos_row = jnp.sum(row_stat[:, 2, 0:1], axis=0, keepdims=True)
    loss_r[r] = jnp.broadcast_to(across(row_lse, half_q) - 2.0 * pos_row, (8, 128))
    loss_z[z] = jnp.broadcast_to(across(col_lse, half_p), (8, 128))
    lrc = [copy(r_dev(d), loss_r.at[r], loss_r.at[r], lr_ss, lr_rs, d) for d in r_range]
    lzc = [copy(z_dev(d), loss_z.at[z], loss_z.at[z], lz_ss, lz_rs, d) for d in z_range]
    for cp in lrc + lzc:
        cp.start()
    dq_recv[z] = dq_send[z]
    dp_recv[r] = dp_send[r]
    for d, cp in zip(z_order, q_copies):
        unless_crossing(d, cp.wait_send)
    if relayed:
        pl.when(z == n_z - 2)(to_last.wait_send)
        pl.when(z == 1)(to_first.wait_send)
    for cp in p_copies + q_shared + p_shared:
        cp.wait_send()

    for cp in dpc:
        cp.wait()
    acc = dp_recv[0].astype(F32)
    for i in r_range:
        acc += dp_recv[i].astype(F32)
    gp_v[...] = (logit_scale * (acc - pair_q[...])).astype(BF16)
    gp_out = pltpu.make_async_copy(gp_v, gp_ref, local_sem.at[3])
    gp_out.start()

    for cp in lrc + lzc:
        cp.wait()
    total = jnp.sum(loss_r[:, 0, 0:1], axis=0, keepdims=True) + jnp.sum(loss_z[:, 0, 0:1], axis=0, keepdims=True)
    loss_v[...] = total / (2.0 * rows * n_row * n_col)
    loss_out = pltpu.make_async_copy(loss_v, loss_ref, local_sem.at[4])
    loss_out.start()

    if relayed:
        pl.when((z == 0) | (z == last))(up.wait_send)
    for d, cp in zip(z_order, dqc):
        unless_crossing(d, cp.wait_send)
        if relayed:
            from_far = ((z == 0) & (d == 1)) | ((z == last) & (d == last))
            pl.when(jnp.logical_not(from_far))(cp.wait_recv)
        else:
            cp.wait_recv()
    acc = dq_recv[0].astype(F32)
    for i in z_range:
        acc += dq_recv[i].astype(F32)
    gq_v[...] = (logit_scale * (acc - pair_p[...])).astype(BF16)
    gq_out = pltpu.make_async_copy(gq_v, gq_ref, local_sem.at[5])
    gq_out.start()
    for cp in (gp_out, loss_out, gq_out):
        cp.wait()


def hand_out(*refs):
    *arrays, sem = refs
    copies = [pltpu.make_async_copy(arrays[i], arrays[i + 3], sem.at[i]) for i in range(3)]
    for cp in copies:
        cp.start()
    for cp in copies:
        cp.wait()


def local(n_row, n_col, query, passage, positive):
    rows, width = query.shape
    n_z = n_col // 2
    dma = pltpu.SemaphoreType.DMA
    loss, gq, gp = pl.pallas_call(
        functools.partial(kernel, n_row, n_col),
        out_shape=(
            pltpu.HBM((1, 1), F32),
            pltpu.HBM((rows, width), BF16),
            pltpu.HBM((rows, width), BF16),
        ),
        in_specs=[pl.BlockSpec(memory_space=pltpu.HBM)] * 3,
        out_specs=[pl.BlockSpec(memory_space=pltpu.HBM)] * 3,
        scratch_shapes=[
            pltpu.VMEM((2, n_z, rows, width), BF16),
            pltpu.VMEM((2, n_row, rows, width), BF16),
            pltpu.VMEM((1, rows), jnp.int32),
            pltpu.VMEM((2, 8, 128), F32),
            pltpu.VMEM((rows, width), F32),
            pltpu.VMEM((rows, width), F32),
            pltpu.VMEM((n_z, 8, 2 * n_z * rows), F32),
            pltpu.VMEM((n_row, 8, 2 * n_row * rows), F32),
            pltpu.VMEM((n_z, rows, width), BF16),
            pltpu.VMEM((n_row, rows, width), BF16),
            pltpu.VMEM((n_z, rows, width), BF16),
            pltpu.VMEM((n_row, rows, width), BF16),
            pltpu.VMEM((rows, width), BF16),
            pltpu.VMEM((n_row, 8, 128), F32),
            pltpu.VMEM((n_z, 8, 128), F32),
            pltpu.VMEM((rows, width), BF16),
            pltpu.VMEM((rows, width), BF16),
            pltpu.VMEM((1, 1), F32),
            dma((6,)),
            dma((n_z,)), dma((n_z,)), dma((n_row,)), dma((n_row,)),
            dma((n_z,)), dma((n_z,)), dma((n_row,)), dma((n_row,)),
            dma((1,)), dma((1,)),
            dma((n_z,)), dma((n_z,)), dma((n_row,)), dma((n_row,)),
            dma((n_z,)), dma((n_z,)), dma((n_row,)), dma((n_row,)),
            dma((n_row,)), dma((n_row,)), dma((n_z,)), dma((n_z,)),
        ],
        compiler_params=pltpu.CompilerParams(
            collective_id=0, has_side_effects=True, vmem_limit_bytes=48 * 1024 * 1024),
    )(*(pltpu.with_memory_space_constraint(x, pltpu.HBM) for x in (query, passage, positive)))
    results = (loss, gq, gp)
    loss, gq, gp = pl.pallas_call(
        hand_out,
        out_shape=tuple(jax.ShapeDtypeStruct(x.shape, x.dtype) for x in results),
        in_specs=[pl.BlockSpec(memory_space=pltpu.HBM)] * 3,
        out_specs=[pl.BlockSpec(memory_space=pltpu.HBM)] * 3,
        scratch_shapes=[dma((3,))],
    )(*(pltpu.with_memory_space_constraint(x, pltpu.HBM) for x in results))
    return loss[0, 0], gq, gp


def solution(mesh):
    return jax.shard_map(
        functools.partial(local, mesh.shape["row"], mesh.shape["col"]),
        mesh=mesh,
        in_specs=(P(("row", "col"), None), P(("row", "col"), None), P(("row", "col"), None)),
        out_specs=(P(), P(("row", "col"), None), P(("row", "col"), None)),
        check_vma=False,
    )
```

```python
import functools

import jax
import jax.numpy as jnp
from jax import lax
from jax.experimental import pallas as pl
from jax.experimental.pallas import tpu as pltpu
from jax.sharding import PartitionSpec as P

logit_scale = 20.0
MESH = pl.DeviceIdType.MESH
F32 = jnp.float32
BF16 = jnp.bfloat16
NT = (((1,), (1,)), ((), ()))
TN = (((0,), (0,)), ((), ()))


def kernel(
    n_row, n_col, q_ref, p_ref, pos_ref, loss_ref, gq_ref, gp_ref,
    q_all, p_all, pos_v, pos_sum, pair_p, pair_q, row_stat, col_stat,
    dq_send, dp_send, dq_recv, dp_recv, loss_r, loss_z,
    local_sem, q_ss, q_rs, p_ss, p_rs, qf_ss, qf_rs, pf_ss, pf_rs, pos_ss, pos_rs,
    rst_ss, rst_rs, cst_ss, cst_rs,
    dq_ss, dq_rs, dp_ss, dp_rs, lr_ss, lr_rs, lz_ss, lz_rs,
):
    rows, width = q_ref.shape
    n_z = n_col // 2
    half_q = n_z * rows
    half_p = n_row * rows
    r = lax.axis_index("row")
    c = lax.axis_index("col")
    z = c // 2
    core = c % 2

    def z_at(d):
        return lax.rem(z + d, n_z)

    def r_at(d):
        return lax.rem(r + d, n_row)

    def z_dev(d):
        return (r, z_at(d) * 2 + core)

    def r_dev(d):
        return (r_at(d), c)

    sibling = (r, z * 2 + 1 - core)

    def copy(device, src, dst, ss, rs, i):
        return pltpu.make_async_remote_copy(
            src_ref=src, dst_ref=dst, send_sem=ss.at[i], recv_sem=rs.at[i],
            device_id=device, device_id_type=MESH)

    z_range = range(1, n_z)
    r_range = range(1, n_row)

    own_p = pltpu.make_async_copy(p_ref, p_all.at[0, r], local_sem.at[0])
    own_q = pltpu.make_async_copy(q_ref, q_all.at[0, z], local_sem.at[1])
    own_pos = pltpu.make_async_copy(pos_ref, pos_v, local_sem.at[2])
    own_p.start()
    own_q.start()
    own_pos.start()

    barrier = pltpu.get_barrier_semaphore()
    for device in [z_dev(d) for d in z_range] + [r_dev(d) for d in r_range] + [sibling]:
        pl.semaphore_signal(barrier, inc=1, device_id=device, device_id_type=MESH)
    pl.semaphore_wait(barrier, n_z + n_row - 1)

    q_copies = [copy(z_dev(d), q_ref, q_all.at[0, z], q_ss, q_rs, d) for d in z_range]
    p_copies = [copy(r_dev(d), p_ref, p_all.at[0, r], p_ss, p_rs, d) for d in r_range]
    q_shared = [copy(sibling, q_ref, q_all.at[1, z], qf_ss, qf_rs, 0)]
    p_shared = [copy(sibling, p_ref, p_all.at[1, r], pf_ss, pf_rs, 0)]
    for cp in q_copies + p_copies + q_shared + p_shared:
        cp.start()

    own_p.wait()
    own_q.wait()
    own_pos.wait()
    q_own = q_all[0, z]
    p_own = p_all[0, r]
    slot = lax.broadcasted_iota(jnp.int32, (rows, rows), 0)
    onehot_t = jnp.where(slot == pos_v[...], 1.0, 0.0).astype(F32)
    paired_p = jnp.dot(onehot_t.T.astype(BF16), p_own, preferred_element_type=F32)
    pair_p[...] = paired_p
    pair_q[...] = jnp.dot(onehot_t.astype(BF16), q_own, preferred_element_type=F32)
    own_sum = logit_scale * jnp.sum(q_own.astype(F32) * paired_p, axis=(0, 1), keepdims=True)
    pos_sum[0] = jnp.broadcast_to(own_sum, (8, 128))
    pos_copy = copy(sibling, pos_sum.at[0], pos_sum.at[1], pos_ss, pos_rs, 0)
    pos_copy.start()

    for d in r_range:
        p_copies[d - 1].wait_recv()
        at = r_at(n_row - d)
        cp = copy(sibling, p_all.at[0, at], p_all.at[1, at], pf_ss, pf_rs, d)
        cp.start()
        p_shared.append(cp)
    for d in z_range:
        q_copies[d - 1].wait_recv()
        at = z_at(n_z - d)
        cp = copy(sibling, q_all.at[0, at], q_all.at[1, at], qf_ss, qf_rs, d)
        cp.start()
        q_shared.append(cp)
    for cp in p_shared + q_shared:
        cp.wait_recv()
    pos_copy.wait()

    q_mat = q_all[...].reshape(2 * half_q, width)
    p_mat = p_all[...].reshape(2 * half_p, width)
    s = logit_scale * lax.dot_general(q_mat, p_mat, NT, preferred_element_type=F32)

    def down(x, half):
        return (jnp.sum(x[:half], axis=0, keepdims=True)
                + jnp.sum(x[half:], axis=0, keepdims=True))

    def across(x, half):
        return (jnp.sum(x[:, :half], axis=1, keepdims=True)
                + jnp.sum(x[:, half:], axis=1, keepdims=True))

    row_peak = jnp.max(s, axis=1, keepdims=True)
    row_exp = jnp.exp(s - row_peak)
    row_sum = across(row_exp, half_p)
    lane = lax.broadcasted_iota(jnp.int32, (2 * half_q, 128), 1)
    pair_sum = pos_sum[0, 0:1, 0:1] + pos_sum[1, 0:1, 0:1]
    row_stat[z] = jnp.where(lane == 0, row_peak, jnp.where(lane == 1, row_sum, pair_sum)).T[0:8]
    rst = [copy(z_dev(d), row_stat.at[z], row_stat.at[z], rst_ss, rst_rs, d) for d in z_range]
    for cp in rst:
        cp.start()
    col_peak = jnp.max(s, axis=0, keepdims=True)
    col_exp = jnp.exp(s - col_peak)
    col_stat[r, 0:1, :] = col_peak
    col_stat[r, 1:2, :] = down(col_exp, half_q)
    cst = [copy(r_dev(d), col_stat.at[r], col_stat.at[r], cst_ss, cst_rs, d) for d in r_range]
    for cp in cst:
        cp.start()
    for cp in cst + rst:
        cp.wait()

    def merge(ref):
        peak = ref[:, 0, :]
        total = ref[:, 1, :]
        top = jnp.max(peak, axis=0, keepdims=True)
        return top + jnp.log(jnp.sum(total * jnp.exp(peak - top), axis=0, keepdims=True))

    row_lse = merge(row_stat)
    col_lse = merge(col_stat)
    row_factor = 0.5 * jnp.exp(row_stat[z, 0:1, :] - row_lse)
    row_mat = jnp.broadcast_to(row_factor, (128, 2 * half_q)).T
    row_mat = jnp.concatenate([row_mat] * (2 * half_p // 128), axis=1)
    col_factor = 0.5 * jnp.exp(col_peak - col_lse)
    w = (row_exp * row_mat + col_exp * col_factor).astype(BF16)

    dq = jnp.dot(w[:half_q], p_mat, preferred_element_type=F32).astype(BF16)
    dq_send[...] = dq.reshape(n_z, rows, width)
    dqc = [copy(z_dev(d), dq_send.at[z_at(d)], dq_recv.at[z], dq_ss, dq_rs, d) for d in z_range]
    for cp in dqc:
        cp.start()
    dp = lax.dot_general(w[:, :half_p], q_mat, TN, preferred_element_type=F32).astype(BF16)
    dp_send[...] = dp.reshape(n_row, rows, width)
    dpc = [copy(r_dev(d), dp_send.at[r_at(d)], dp_recv.at[r], dp_ss, dp_rs, d) for d in r_range]
    for cp in dpc:
        cp.start()
    pos_row = jnp.sum(row_stat[:, 2, 0:1], axis=0, keepdims=True)
    loss_r[r] = jnp.broadcast_to(across(row_lse, half_q) - 2.0 * pos_row, (8, 128))
    loss_z[z] = jnp.broadcast_to(across(col_lse, half_p), (8, 128))
    lrc = [copy(r_dev(d), loss_r.at[r], loss_r.at[r], lr_ss, lr_rs, d) for d in r_range]
    lzc = [copy(z_dev(d), loss_z.at[z], loss_z.at[z], lz_ss, lz_rs, d) for d in z_range]
    for cp in lrc + lzc:
        cp.start()
    dq_recv[z] = dq_send[z]
    dp_recv[r] = dp_send[r]
    for cp in q_copies + p_copies + q_shared + p_shared:
        cp.wait_send()

    for cp in dpc:
        cp.wait()
    acc = dp_recv[0].astype(F32)
    for i in r_range:
        acc += dp_recv[i].astype(F32)
    gp_ref[...] = (logit_scale * (acc - pair_q[...])).astype(BF16)

    for cp in lrc + lzc:
        cp.wait()
    total = jnp.sum(loss_r[:, 0, 0:1], axis=0, keepdims=True) + jnp.sum(loss_z[:, 0, 0:1], axis=0, keepdims=True)
    loss_ref[...] = jnp.broadcast_to(total / (2.0 * rows * n_row * n_col), (8, 128))

    for cp in dqc:
        cp.wait()
    acc = dq_recv[0].astype(F32)
    for i in z_range:
        acc += dq_recv[i].astype(F32)
    gq_ref[...] = (logit_scale * (acc - pair_p[...])).astype(BF16)


def hand_out(loss_ref, gq_ref, gp_ref, loss_out, gq_out, gp_out, loss_v, sem):
    loss_v[...] = loss_ref[0:1, 0:1]
    pairs = ((gq_ref, gq_out), (gp_ref, gp_out), (loss_v, loss_out))
    copies = [pltpu.make_async_copy(src, dst, sem.at[i]) for i, (src, dst) in enumerate(pairs)]
    for cp in copies:
        cp.start()
    for cp in copies:
        cp.wait()


def local(n_row, n_col, query, passage, positive):
    rows, width = query.shape
    n_z = n_col // 2
    dma = pltpu.SemaphoreType.DMA
    loss, gq, gp = pl.pallas_call(
        functools.partial(kernel, n_row, n_col),
        out_shape=(
            pltpu.VMEM((8, 128), F32),
            pltpu.VMEM((rows, width), BF16),
            pltpu.VMEM((rows, width), BF16),
        ),
        in_specs=[pl.BlockSpec(memory_space=pltpu.HBM)] * 3,
        out_specs=[pl.BlockSpec(memory_space=pltpu.VMEM)] * 3,
        scratch_shapes=[
            pltpu.VMEM((2, n_z, rows, width), BF16),
            pltpu.VMEM((2, n_row, rows, width), BF16),
            pltpu.VMEM((1, rows), jnp.int32),
            pltpu.VMEM((2, 8, 128), F32),
            pltpu.VMEM((rows, width), F32),
            pltpu.VMEM((rows, width), F32),
            pltpu.VMEM((n_z, 8, 2 * n_z * rows), F32),
            pltpu.VMEM((n_row, 8, 2 * n_row * rows), F32),
            pltpu.VMEM((n_z, rows, width), BF16),
            pltpu.VMEM((n_row, rows, width), BF16),
            pltpu.VMEM((n_z, rows, width), BF16),
            pltpu.VMEM((n_row, rows, width), BF16),
            pltpu.VMEM((n_row, 8, 128), F32),
            pltpu.VMEM((n_z, 8, 128), F32),
            dma((3,)),
            dma((n_z,)), dma((n_z,)), dma((n_row,)), dma((n_row,)),
            dma((n_z,)), dma((n_z,)), dma((n_row,)), dma((n_row,)),
            dma((1,)), dma((1,)),
            dma((n_z,)), dma((n_z,)), dma((n_row,)), dma((n_row,)),
            dma((n_z,)), dma((n_z,)), dma((n_row,)), dma((n_row,)),
            dma((n_row,)), dma((n_row,)), dma((n_z,)), dma((n_z,)),
        ],
        compiler_params=pltpu.CompilerParams(
            collective_id=0, has_side_effects=True, vmem_limit_bytes=48 * 1024 * 1024),
    )(*(pltpu.with_memory_space_constraint(x, pltpu.HBM) for x in (query, passage, positive)))
    loss, gq, gp = pl.pallas_call(
        hand_out,
        out_shape=(
            jax.ShapeDtypeStruct((1, 1), F32),
            jax.ShapeDtypeStruct(gq.shape, BF16),
            jax.ShapeDtypeStruct(gp.shape, BF16),
        ),
        in_specs=[pl.BlockSpec(memory_space=pltpu.VMEM)] * 3,
        out_specs=[pl.BlockSpec(memory_space=pl.ANY)] * 3,
        scratch_shapes=[pltpu.VMEM((1, 1), F32), dma((3,))],
    )(*(pltpu.with_memory_space_constraint(x, pltpu.VMEM) for x in (loss, gq, gp)))
    return loss[0, 0], gq, gp


def solution(mesh):
    return jax.shard_map(
        functools.partial(local, mesh.shape["row"], mesh.shape["col"]),
        mesh=mesh,
        in_specs=(P(("row", "col"), None), P(("row", "col"), None), P(("row", "col"), None)),
        out_specs=(P(), P(("row", "col"), None), P(("row", "col"), None)),
        check_vma=False,
    )
```

```python
import functools

import jax
import jax.numpy as jnp
from jax import lax
from jax.experimental import pallas as pl
from jax.experimental.pallas import tpu as pltpu
from jax.sharding import PartitionSpec as P

logit_scale = 20.0
MESH = pl.DeviceIdType.MESH
F32 = jnp.float32
BF16 = jnp.bfloat16
NT = (((1,), (1,)), ((), ()))
TN = (((0,), (0,)), ((), ()))


def kernel(
    n_row, n_col, q_ref, p_ref, pos_ref, loss_ref, gq_ref, gp_ref,
    q_all, p_all, pos_v, pos_sum, pair_p, pair_q, row_stat, col_stat,
    dq_send, dp_send, dq_recv, dp_recv, loss_r, loss_z,
    s_v, row_exp, col_exp, stat_cols, w_q, w_p,
    local_sem, q_ss, q_rs, p_ss, p_rs, qf_ss, qf_rs, pf_ss, pf_rs, pos_ss, pos_rs,
    rst_ss, rst_rs, cst_ss, cst_rs,
    dq_ss, dq_rs, dp_ss, dp_rs, lr_ss, lr_rs, lz_ss, lz_rs,
):
    rows, width = q_ref.shape
    n_z = n_col // 2
    half_q = n_z * rows
    half_p = n_row * rows
    n_q, n_p = 2 * half_q, 2 * half_p
    step = 256
    block = 64
    r = lax.axis_index("row")
    c = lax.axis_index("col")
    z = c // 2
    core = c % 2

    def z_at(d):
        return lax.rem(z + d, n_z)

    def r_at(d):
        return lax.rem(r + d, n_row)

    def z_dev(d):
        return (r, z_at(d) * 2 + core)

    def r_dev(d):
        return (r_at(d), c)

    sibling = (r, z * 2 + 1 - core)

    def copy(device, src, dst, ss, rs, i):
        return pltpu.make_async_remote_copy(
            src_ref=src, dst_ref=dst, send_sem=ss.at[i], recv_sem=rs.at[i],
            device_id=device, device_id_type=MESH)

    z_range = range(1, n_z)
    r_range = range(1, n_row)

    own_p = pltpu.make_async_copy(p_ref, p_all.at[0, r], local_sem.at[0])
    own_q = pltpu.make_async_copy(q_ref, q_all.at[0, z], local_sem.at[1])
    own_pos = pltpu.make_async_copy(pos_ref, pos_v, local_sem.at[2])
    own_p.start()
    own_q.start()
    own_pos.start()

    barrier = pltpu.get_barrier_semaphore()
    for device in [z_dev(d) for d in z_range] + [r_dev(d) for d in r_range] + [sibling]:
        pl.semaphore_signal(barrier, inc=1, device_id=device, device_id_type=MESH)
    pl.semaphore_wait(barrier, n_z + n_row - 1)

    q_copies = [copy(z_dev(d), q_ref, q_all.at[0, z], q_ss, q_rs, d) for d in z_range]
    p_copies = [copy(r_dev(d), p_ref, p_all.at[0, r], p_ss, p_rs, d) for d in r_range]
    q_shared = [copy(sibling, q_ref, q_all.at[1, z], qf_ss, qf_rs, 0)]
    p_shared = [copy(sibling, p_ref, p_all.at[1, r], pf_ss, pf_rs, 0)]
    for cp in q_copies + p_copies + q_shared + p_shared:
        cp.start()

    own_p.wait()
    own_q.wait()
    own_pos.wait()
    slot = lax.broadcasted_iota(jnp.int32, (rows, rows), 0)
    onehot_t = jnp.where(slot == pos_v[...], 1.0, 0.0).astype(F32)
    by_query = onehot_t.T.astype(BF16)
    by_passage = onehot_t.astype(BF16)

    def pair_step(i, total):
        cols = pl.ds(pl.multiple_of(i * step, step), step)
        q_part = q_all[0, z, :, cols]
        paired = jnp.dot(by_query, p_all[0, r, :, cols], preferred_element_type=F32)
        pair_p[:, cols] = paired
        pair_q[:, cols] = jnp.dot(by_passage, q_part, preferred_element_type=F32)
        return total + q_part.astype(F32) * paired

    products = lax.fori_loop(0, width // step, pair_step, jnp.zeros((rows, step), F32))
    own_sum = logit_scale * jnp.sum(products, axis=(0, 1), keepdims=True)
    pos_sum[0] = jnp.broadcast_to(own_sum, (8, 128))
    pos_copy = copy(sibling, pos_sum.at[0], pos_sum.at[1], pos_ss, pos_rs, 0)
    pos_copy.start()

    for d in r_range:
        p_copies[d - 1].wait_recv()
        at = r_at(n_row - d)
        cp = copy(sibling, p_all.at[0, at], p_all.at[1, at], pf_ss, pf_rs, d)
        cp.start()
        p_shared.append(cp)
    for d in z_range:
        q_copies[d - 1].wait_recv()
        at = z_at(n_z - d)
        cp = copy(sibling, q_all.at[0, at], q_all.at[1, at], qf_ss, qf_rs, d)
        cp.start()
        q_shared.append(cp)
    for cp in p_shared + q_shared:
        cp.wait_recv()
    pos_copy.wait()

    def score_step(i, carry):
        cols = pl.ds(pl.multiple_of(i * step, step), step)
        part = lax.dot_general(
            q_all[:, :, :, cols].reshape(n_q, step), p_all[:, :, :, cols].reshape(n_p, step),
            NT, preferred_element_type=F32)

        @pl.when(i == 0)
        def _():
            s_v[...] = part

        @pl.when(i > 0)
        def _():
            s_v[...] += part
        return carry

    lax.fori_loop(0, width // step, score_step, 0)

    def across(x, half):
        return (jnp.sum(x[:, :half], axis=1, keepdims=True)
                + jnp.sum(x[:, half:], axis=1, keepdims=True))

    lane = lax.broadcasted_iota(jnp.int32, (block, 128), 1)
    pair_sum = pos_sum[0, 0:1, 0:1] + pos_sum[1, 0:1, 0:1]

    def row_step(i, peak):
        at = pl.ds(pl.multiple_of(i * block, block), block)
        x = logit_scale * s_v[at, :]
        s_v[at, :] = x
        row_peak = jnp.max(x, axis=1, keepdims=True)
        e = jnp.exp(x - row_peak)
        row_exp[at, :] = e
        row_sum = across(e, half_p)
        stat_cols[at, :] = jnp.where(lane == 0, row_peak, jnp.where(lane == 1, row_sum, pair_sum))
        return jnp.maximum(peak, jnp.max(x, axis=0, keepdims=True))

    col_peak = lax.fori_loop(0, n_q // block, row_step, jnp.full((1, n_p), -jnp.inf, F32))
    row_stat[z] = stat_cols[...].T[0:8]
    rst = [copy(z_dev(d), row_stat.at[z], row_stat.at[z], rst_ss, rst_rs, d) for d in z_range]
    for cp in rst:
        cp.start()

    def col_step(i, total):
        at = pl.ds(pl.multiple_of(i * block, block), block)
        e = jnp.exp(s_v[at, :] - col_peak)
        col_exp[at, :] = e
        return total + jnp.sum(e, axis=0, keepdims=True)

    per_half = half_q // block
    zero = jnp.zeros((1, n_p), F32)
    col_sum = (lax.fori_loop(0, per_half, col_step, zero)
               + lax.fori_loop(per_half, 2 * per_half, col_step, zero))
    col_stat[r, 0:1, :] = col_peak
    col_stat[r, 1:2, :] = col_sum
    cst = [copy(r_dev(d), col_stat.at[r], col_stat.at[r], cst_ss, cst_rs, d) for d in r_range]
    for cp in cst:
        cp.start()
    for cp in cst + rst:
        cp.wait()

    def merge(ref):
        peak = ref[:, 0, :]
        total = ref[:, 1, :]
        top = jnp.max(peak, axis=0, keepdims=True)
        return top + jnp.log(jnp.sum(total * jnp.exp(peak - top), axis=0, keepdims=True))

    row_lse = merge(row_stat)
    col_lse = merge(col_stat)
    row_factor = 0.5 * jnp.exp(row_stat[z, 0:1, :] - row_lse)
    stat_cols[...] = jnp.broadcast_to(row_factor, (128, n_q)).T
    col_factor = 0.5 * jnp.exp(col_peak - col_lse)

    def weight_step(i, carry):
        at = pl.ds(pl.multiple_of(i * block, block), block)
        factor = jnp.concatenate([stat_cols[at, :]] * (n_p // 128), axis=1)
        s_v[at, :] = row_exp[at, :] * factor + col_exp[at, :] * col_factor
        return carry

    lax.fori_loop(0, n_q // block, weight_step, 0)
    w_q[...] = s_v[0:half_q, :].astype(BF16)
    w_p[...] = s_v[:, 0:half_p].T.astype(BF16)

    def dq_step(i, carry):
        cols = pl.ds(pl.multiple_of(i * step, step), step)
        dq = jnp.dot(w_q[...], p_all[:, :, :, cols].reshape(n_p, step), preferred_element_type=F32)
        dq_send[:, :, cols] = dq.astype(BF16).reshape(n_z, rows, step)
        return carry

    lax.fori_loop(0, width // step, dq_step, 0)
    dqc = [copy(z_dev(d), dq_send.at[z_at(d)], dq_recv.at[z], dq_ss, dq_rs, d) for d in z_range]
    for cp in dqc:
        cp.start()

    def dp_step(i, carry):
        cols = pl.ds(pl.multiple_of(i * step, step), step)
        dp = jnp.dot(w_p[...], q_all[:, :, :, cols].reshape(n_q, step), preferred_element_type=F32)
        dp_send[:, :, cols] = dp.astype(BF16).reshape(n_row, rows, step)
        return carry

    lax.fori_loop(0, width // step, dp_step, 0)
    dpc = [copy(r_dev(d), dp_send.at[r_at(d)], dp_recv.at[r], dp_ss, dp_rs, d) for d in r_range]
    for cp in dpc:
        cp.start()
    pos_row = jnp.sum(row_stat[:, 2, 0:1], axis=0, keepdims=True)
    loss_r[r] = jnp.broadcast_to(across(row_lse, half_q) - 2.0 * pos_row, (8, 128))
    loss_z[z] = jnp.broadcast_to(across(col_lse, half_p), (8, 128))
    lrc = [copy(r_dev(d), loss_r.at[r], loss_r.at[r], lr_ss, lr_rs, d) for d in r_range]
    lzc = [copy(z_dev(d), loss_z.at[z], loss_z.at[z], lz_ss, lz_rs, d) for d in z_range]
    for cp in lrc + lzc:
        cp.start()
    dq_recv[z] = dq_send[z]
    dp_recv[r] = dp_send[r]
    for cp in q_copies + p_copies + q_shared + p_shared:
        cp.wait_send()

    for cp in dpc:
        cp.wait()
    def add_up(terms, paired, out, count):
        def body(i, carry):
            cols = pl.ds(pl.multiple_of(i * step, step), step)
            acc = terms[0, :, cols].astype(F32)
            for j in range(1, count):
                acc += terms[j, :, cols].astype(F32)
            out[:, cols] = (logit_scale * (acc - paired[:, cols])).astype(BF16)
            return carry
        lax.fori_loop(0, width // step, body, 0)

    add_up(dp_recv, pair_q, gp_ref, n_row)

    for cp in lrc + lzc:
        cp.wait()
    total = jnp.sum(loss_r[:, 0, 0:1], axis=0, keepdims=True) + jnp.sum(loss_z[:, 0, 0:1], axis=0, keepdims=True)
    loss_ref[...] = jnp.broadcast_to(total / (2.0 * rows * n_row * n_col), (8, 128))

    for cp in dqc:
        cp.wait()
    add_up(dq_recv, pair_p, gq_ref, n_z)


def hand_out(loss_ref, gq_ref, gp_ref, loss_out, gq_out, gp_out, loss_v, sem):
    loss_v[...] = loss_ref[0:1, 0:1]
    pairs = ((gq_ref, gq_out), (gp_ref, gp_out), (loss_v, loss_out))
    copies = [pltpu.make_async_copy(src, dst, sem.at[i]) for i, (src, dst) in enumerate(pairs)]
    for cp in copies:
        cp.start()
    for cp in copies:
        cp.wait()


def local(n_row, n_col, query, passage, positive):
    rows, width = query.shape
    n_z = n_col // 2
    n_q, n_p = 2 * n_z * rows, 2 * n_row * rows
    dma = pltpu.SemaphoreType.DMA
    loss, gq, gp = pl.pallas_call(
        functools.partial(kernel, n_row, n_col),
        out_shape=(
            pltpu.VMEM((8, 128), F32),
            pltpu.VMEM((rows, width), BF16),
            pltpu.VMEM((rows, width), BF16),
        ),
        in_specs=[pl.BlockSpec(memory_space=pltpu.HBM)] * 3,
        out_specs=[pl.BlockSpec(memory_space=pltpu.VMEM)] * 3,
        scratch_shapes=[
            pltpu.VMEM((2, n_z, rows, width), BF16),
            pltpu.VMEM((2, n_row, rows, width), BF16),
            pltpu.VMEM((1, rows), jnp.int32),
            pltpu.VMEM((2, 8, 128), F32),
            pltpu.VMEM((rows, width), F32),
            pltpu.VMEM((rows, width), F32),
            pltpu.VMEM((n_z, 8, 2 * n_z * rows), F32),
            pltpu.VMEM((n_row, 8, 2 * n_row * rows), F32),
            pltpu.VMEM((n_z, rows, width), BF16),
            pltpu.VMEM((n_row, rows, width), BF16),
            pltpu.VMEM((n_z, rows, width), BF16),
            pltpu.VMEM((n_row, rows, width), BF16),
            pltpu.VMEM((n_row, 8, 128), F32),
            pltpu.VMEM((n_z, 8, 128), F32),
            pltpu.VMEM((n_q, n_p), F32),
            pltpu.VMEM((n_q, n_p), F32),
            pltpu.VMEM((n_q, n_p), F32),
            pltpu.VMEM((n_q, 128), F32),
            pltpu.VMEM((n_q // 2, n_p), BF16),
            pltpu.VMEM((n_p // 2, n_q), BF16),
            dma((3,)),
            dma((n_z,)), dma((n_z,)), dma((n_row,)), dma((n_row,)),
            dma((n_z,)), dma((n_z,)), dma((n_row,)), dma((n_row,)),
            dma((1,)), dma((1,)),
            dma((n_z,)), dma((n_z,)), dma((n_row,)), dma((n_row,)),
            dma((n_z,)), dma((n_z,)), dma((n_row,)), dma((n_row,)),
            dma((n_row,)), dma((n_row,)), dma((n_z,)), dma((n_z,)),
        ],
        compiler_params=pltpu.CompilerParams(
            collective_id=0, has_side_effects=True, vmem_limit_bytes=48 * 1024 * 1024),
    )(*(pltpu.with_memory_space_constraint(x, pltpu.HBM) for x in (query, passage, positive)))
    loss, gq, gp = pl.pallas_call(
        hand_out,
        out_shape=(
            jax.ShapeDtypeStruct((1, 1), F32),
            jax.ShapeDtypeStruct(gq.shape, BF16),
            jax.ShapeDtypeStruct(gp.shape, BF16),
        ),
        in_specs=[pl.BlockSpec(memory_space=pltpu.VMEM)] * 3,
        out_specs=[pl.BlockSpec(memory_space=pl.ANY)] * 3,
        scratch_shapes=[pltpu.VMEM((1, 1), F32), dma((3,))],
    )(*(pltpu.with_memory_space_constraint(x, pltpu.VMEM) for x in (loss, gq, gp)))
    return loss[0, 0], gq, gp


def solution(mesh):
    return jax.shard_map(
        functools.partial(local, mesh.shape["row"], mesh.shape["col"]),
        mesh=mesh,
        in_specs=(P(("row", "col"), None), P(("row", "col"), None), P(("row", "col"), None)),
        out_specs=(P(), P(("row", "col"), None), P(("row", "col"), None)),
        check_vma=False,
    )
```

```python
import functools

import jax
import jax.numpy as jnp
from jax import lax
from jax.experimental import pallas as pl
from jax.experimental.pallas import tpu as pltpu
from jax.sharding import PartitionSpec as P

logit_scale = 20.0
MESH = pl.DeviceIdType.MESH
F32 = jnp.float32
BF16 = jnp.bfloat16
NT = (((1,), (1,)), ((), ()))
TN = (((0,), (0,)), ((), ()))


def kernel(
    n_row, n_col, q_ref, p_ref, pos_ref, loss_ref, gq_ref, gp_ref,
    q_all, p_all, pos_v, pair_p, pair_q, row_stat, col_stat, col_swap, w_sent, w_got,
    dq_send, dp_send, dq_recv, dp_recv, loss_r, loss_z,
    local_sem, q_ss, q_rs, p_ss, p_rs, qf_ss, qf_rs, pf_ss, pf_rs, w_ss, w_rs,
    rst_ss, rst_rs, cst_ss, cst_rs,
    dq_ss, dq_rs, dp_ss, dp_rs, lr_ss, lr_rs, lz_ss, lz_rs,
):
    rows, width = q_ref.shape
    n_z = n_col // 2
    half_q = n_z * rows
    half_p = n_row * rows
    r = lax.axis_index("row")
    c = lax.axis_index("col")
    z = c // 2
    core = c % 2
    g = r * 2 + core
    n_g = n_row * 2

    def z_at(d):
        return lax.rem(z + d, n_z)

    def r_at(d):
        return lax.rem(r + d, n_row)

    def z_dev(d):
        return (r, z_at(d) * 2 + core)

    def r_dev(d):
        return (r_at(d), c)

    def g_dev(d):
        gg = lax.rem(g + d, n_g)
        return (gg // 2, z * 2 + gg % 2)

    sibling = (r, z * 2 + 1 - core)

    def copy(device, src, dst, ss, rs, i):
        return pltpu.make_async_remote_copy(
            src_ref=src, dst_ref=dst, send_sem=ss.at[i], recv_sem=rs.at[i],
            device_id=device, device_id_type=MESH)

    z_range = range(1, n_z)
    r_range = range(1, n_row)
    g_range = range(1, n_g)

    own_p = pltpu.make_async_copy(p_ref, p_all.at[0, r], local_sem.at[0])
    own_q = pltpu.make_async_copy(q_ref, q_all.at[0, z], local_sem.at[1])
    own_pos = pltpu.make_async_copy(pos_ref, pos_v, local_sem.at[2])
    own_p.start()
    own_q.start()
    own_pos.start()

    barrier = pltpu.get_barrier_semaphore()
    for device in [z_dev(d) for d in z_range] + [g_dev(d) for d in g_range]:
        pl.semaphore_signal(barrier, inc=1, device_id=device, device_id_type=MESH)
    pl.semaphore_wait(barrier, n_z - 1 + n_g - 1)

    q_copies = [copy(z_dev(d), q_ref, q_all.at[0, z], q_ss, q_rs, d) for d in z_range]
    p_copies = [copy(r_dev(d), p_ref, p_all.at[0, r], p_ss, p_rs, d) for d in r_range]
    p_shared = [copy(sibling, p_ref, p_all.at[1, r], pf_ss, pf_rs, 0)]
    for cp in q_copies + p_copies + p_shared:
        cp.start()

    own_p.wait()
    own_q.wait()
    own_pos.wait()
    q_own = q_all[0, z]
    p_own = p_all[0, r]
    slot = lax.broadcasted_iota(jnp.int32, (rows, rows), 0)
    onehot_t = jnp.where(slot == pos_v[...], 1.0, 0.0).astype(F32)
    paired_p = jnp.dot(onehot_t.T.astype(BF16), p_own, preferred_element_type=F32)
    pair_p[...] = paired_p
    pair_q[...] = jnp.dot(onehot_t.astype(BF16), q_own, preferred_element_type=F32)
    own_sum = logit_scale * jnp.sum(q_own.astype(F32) * paired_p, axis=(0, 1), keepdims=True)
    for d in r_range:
        p_copies[d - 1].wait_recv()
        at = r_at(n_row - d)
        cp = copy(sibling, p_all.at[0, at], p_all.at[1, at], pf_ss, pf_rs, d)
        cp.start()
        p_shared.append(cp)
    for cp in p_shared:
        cp.wait_recv()
    for cp in q_copies:
        cp.wait_recv()

    q_mat = q_all[0].reshape(half_q, width)
    p_mat = p_all[...].reshape(2 * half_p, width)
    s = logit_scale * lax.dot_general(q_mat, p_mat, NT, preferred_element_type=F32)

    s_t = logit_scale * lax.dot_general(p_mat, q_mat, NT, preferred_element_type=F32)

    def across(x, half):
        return (jnp.sum(x[:, :half], axis=1, keepdims=True)
                + jnp.sum(x[:, half:], axis=1, keepdims=True))

    row_peak = jnp.max(s_t, axis=0, keepdims=True)
    row_stat[z, 0:1, :] = row_peak
    row_stat[z, 1:2, :] = jnp.sum(jnp.exp(s_t - row_peak), axis=0, keepdims=True)
    row_stat[z, 2:3, :] = jnp.broadcast_to(own_sum, (1, half_q))
    rst = [copy(z_dev(d), row_stat.at[z], row_stat.at[z], rst_ss, rst_rs, d) for d in z_range]
    for cp in rst:
        cp.start()
    col_peak = jnp.max(s, axis=0, keepdims=True)
    col_exp = jnp.exp(s - col_peak)
    col_sum = jnp.sum(col_exp, axis=0, keepdims=True)
    col_stat[g, 0:1, :] = col_peak
    col_stat[g, 1:2, :] = col_sum
    col_swap[0:1, :half_p] = col_peak[:, half_p:]
    col_swap[0:1, half_p:] = col_peak[:, :half_p]
    col_swap[1:2, :half_p] = col_sum[:, half_p:]
    col_swap[1:2, half_p:] = col_sum[:, :half_p]
    cst = [copy(g_dev(d), col_swap if d % 2 else col_stat.at[g], col_stat.at[g], cst_ss, cst_rs, d)
           for d in g_range]
    for cp in cst:
        cp.start()
    q_shared = copy(sibling, q_all.at[0], q_all.at[1], qf_ss, qf_rs, 0)
    q_shared.start()
    for cp in cst + rst:
        cp.wait()

    def merge(ref):
        peak = ref[:, 0, :]
        total = ref[:, 1, :]
        top = jnp.max(peak, axis=0, keepdims=True)
        return top + jnp.log(jnp.sum(total * jnp.exp(peak - top), axis=0, keepdims=True))

    row_lse = merge(row_stat)
    col_lse = merge(col_stat)
    row_mat = jnp.broadcast_to(row_lse, (128, half_q)).T
    row_mat = jnp.concatenate([row_mat] * (2 * half_p // 128), axis=1)
    col_factor = 0.5 * jnp.exp(col_peak - col_lse)
    w = 0.5 * jnp.exp(s - row_mat) + col_exp * col_factor
    w_t = w.T.astype(BF16)
    w_sent[...] = w_t[half_p:]
    w_copy = copy(sibling, w_sent, w_got, w_ss, w_rs, 0)
    w_copy.start()

    dq = jnp.dot(w.astype(BF16), p_mat, preferred_element_type=F32).astype(BF16)
    dq_send[...] = dq.reshape(n_z, rows, width)
    dqc = [copy(z_dev(d), dq_send.at[z_at(d)], dq_recv.at[z], dq_ss, dq_rs, d) for d in z_range]
    for cp in dqc:
        cp.start()
    q_shared.wait()
    w_copy.wait()
    w_both = jnp.concatenate([w_t[:half_p], w_got[...]], axis=1)
    q_both = q_all[...].reshape(2 * half_q, width)
    dp = jnp.dot(w_both, q_both, preferred_element_type=F32).astype(BF16)
    dp_send[...] = dp.reshape(n_row, rows, width)
    dpc = [copy(r_dev(d), dp_send.at[r_at(d)], dp_recv.at[r], dp_ss, dp_rs, d) for d in r_range]
    for cp in dpc:
        cp.start()
    pos_row = jnp.sum(row_stat[:, 2, 0:1], axis=0, keepdims=True)
    loss_r[g] = jnp.broadcast_to(jnp.sum(row_lse, axis=1, keepdims=True) - 2.0 * pos_row, (8, 128))
    loss_z[z] = jnp.broadcast_to(across(col_lse, half_p), (8, 128))
    lrc = [copy(g_dev(d), loss_r.at[g], loss_r.at[g], lr_ss, lr_rs, d) for d in g_range]
    lzc = [copy(z_dev(d), loss_z.at[z], loss_z.at[z], lz_ss, lz_rs, d) for d in z_range]
    for cp in lrc + lzc:
        cp.start()
    dq_recv[z] = dq_send[z]
    dp_recv[r] = dp_send[r]
    for cp in q_copies + p_copies + p_shared:
        cp.wait_send()

    for cp in dpc:
        cp.wait()
    acc = dp_recv[0].astype(F32)
    for i in r_range:
        acc += dp_recv[i].astype(F32)
    gp_ref[...] = (logit_scale * (acc - pair_q[...])).astype(BF16)

    for cp in lrc + lzc:
        cp.wait()
    total = jnp.sum(loss_r[:, 0, 0:1], axis=0, keepdims=True) + jnp.sum(loss_z[:, 0, 0:1], axis=0, keepdims=True)
    loss_ref[...] = jnp.broadcast_to(total / (2.0 * rows * n_row * n_col), (8, 128))

    for cp in dqc:
        cp.wait()
    acc = dq_recv[0].astype(F32)
    for i in z_range:
        acc += dq_recv[i].astype(F32)
    gq_ref[...] = (logit_scale * (acc - pair_p[...])).astype(BF16)


def hand_out(loss_ref, gq_ref, gp_ref, loss_out, gq_out, gp_out, loss_v, sem):
    loss_v[...] = loss_ref[0:1, 0:1]
    pairs = ((gq_ref, gq_out), (gp_ref, gp_out), (loss_v, loss_out))
    copies = [pltpu.make_async_copy(src, dst, sem.at[i]) for i, (src, dst) in enumerate(pairs)]
    for cp in copies:
        cp.start()
    for cp in copies:
        cp.wait()


def local(n_row, n_col, query, passage, positive):
    rows, width = query.shape
    n_z, n_g = n_col // 2, n_row * 2
    dma = pltpu.SemaphoreType.DMA
    loss, gq, gp = pl.pallas_call(
        functools.partial(kernel, n_row, n_col),
        out_shape=(
            pltpu.VMEM((8, 128), F32),
            pltpu.VMEM((rows, width), BF16),
            pltpu.VMEM((rows, width), BF16),
        ),
        in_specs=[pl.BlockSpec(memory_space=pltpu.HBM)] * 3,
        out_specs=[pl.BlockSpec(memory_space=pltpu.VMEM)] * 3,
        scratch_shapes=[
            pltpu.VMEM((2, n_z, rows, width), BF16),
            pltpu.VMEM((2, n_row, rows, width), BF16),
            pltpu.VMEM((1, rows), jnp.int32),
            pltpu.VMEM((rows, width), F32),
            pltpu.VMEM((rows, width), F32),
            pltpu.VMEM((n_z, 8, n_z * rows), F32),
            pltpu.VMEM((n_g, 8, n_g * rows), F32),
            pltpu.VMEM((8, n_g * rows), F32),
            pltpu.VMEM((n_row * rows, n_z * rows), BF16),
            pltpu.VMEM((n_row * rows, n_z * rows), BF16),
            pltpu.VMEM((n_z, rows, width), BF16),
            pltpu.VMEM((n_row, rows, width), BF16),
            pltpu.VMEM((n_z, rows, width), BF16),
            pltpu.VMEM((n_row, rows, width), BF16),
            pltpu.VMEM((n_g, 8, 128), F32),
            pltpu.VMEM((n_z, 8, 128), F32),
            dma((3,)),
            dma((n_z,)), dma((n_z,)), dma((n_row,)), dma((n_row,)),
            dma((1,)), dma((1,)), dma((n_row,)), dma((n_row,)),
            dma((1,)), dma((1,)),
            dma((n_z,)), dma((n_z,)), dma((n_g,)), dma((n_g,)),
            dma((n_z,)), dma((n_z,)), dma((n_row,)), dma((n_row,)),
            dma((n_g,)), dma((n_g,)), dma((n_z,)), dma((n_z,)),
        ],
        compiler_params=pltpu.CompilerParams(
            collective_id=0, has_side_effects=True, vmem_limit_bytes=48 * 1024 * 1024),
    )(*(pltpu.with_memory_space_constraint(x, pltpu.HBM) for x in (query, passage, positive)))
    loss, gq, gp = pl.pallas_call(
        hand_out,
        out_shape=(
            jax.ShapeDtypeStruct((1, 1), F32),
            jax.ShapeDtypeStruct(gq.shape, BF16),
            jax.ShapeDtypeStruct(gp.shape, BF16),
        ),
        in_specs=[pl.BlockSpec(memory_space=pltpu.VMEM)] * 3,
        out_specs=[pl.BlockSpec(memory_space=pl.ANY)] * 3,
        scratch_shapes=[pltpu.VMEM((1, 1), F32), dma((3,))],
    )(*(pltpu.with_memory_space_constraint(x, pltpu.VMEM) for x in (loss, gq, gp)))
    return loss[0, 0], gq, gp


def solution(mesh):
    return jax.shard_map(
        functools.partial(local, mesh.shape["row"], mesh.shape["col"]),
        mesh=mesh,
        in_specs=(P(("row", "col"), None), P(("row", "col"), None), P(("row", "col"), None)),
        out_specs=(P(), P(("row", "col"), None), P(("row", "col"), None)),
        check_vma=False,
    )
```

```python
import functools

import jax
import jax.numpy as jnp
from jax import lax
from jax.experimental import pallas as pl
from jax.experimental.pallas import tpu as pltpu
from jax.sharding import PartitionSpec as P

logit_scale = 20.0
MESH = pl.DeviceIdType.MESH
F32 = jnp.float32
BF16 = jnp.bfloat16
NT = (((1,), (1,)), ((), ()))
TN = (((0,), (0,)), ((), ()))


def kernel(
    n_row, n_col, q_ref, p_ref, pos_ref, loss_ref, gq_ref, gp_ref,
    q_all, p_all, pos_v, pair_p, pair_q, row_stat, col_stat, col_swap, w_sent, w_got,
    dq_send, dp_send, dq_recv, dp_recv, loss_r, loss_z,
    local_sem, q_ss, q_rs, p_ss, p_rs, qf_ss, qf_rs, pf_ss, pf_rs, w_ss, w_rs,
    rst_ss, rst_rs, cst_ss, cst_rs,
    dq_ss, dq_rs, dp_ss, dp_rs, lr_ss, lr_rs, lz_ss, lz_rs,
):
    rows, width = q_ref.shape
    n_z = n_col // 2
    half_q = n_z * rows
    half_p = n_row * rows
    r = lax.axis_index("row")
    c = lax.axis_index("col")
    z = c // 2
    core = c % 2
    g = r * 2 + core
    n_g = n_row * 2

    def z_at(d):
        return lax.rem(z + d, n_z)

    def r_at(d):
        return lax.rem(r + d, n_row)

    def z_dev(d):
        return (r, z_at(d) * 2 + core)

    def r_dev(d):
        return (r_at(d), c)

    def g_dev(d):
        gg = lax.rem(g + d, n_g)
        return (gg // 2, z * 2 + gg % 2)

    sibling = (r, z * 2 + 1 - core)

    def copy(device, src, dst, ss, rs, i):
        return pltpu.make_async_remote_copy(
            src_ref=src, dst_ref=dst, send_sem=ss.at[i], recv_sem=rs.at[i],
            device_id=device, device_id_type=MESH)

    z_range = range(1, n_z)
    r_range = range(1, n_row)
    g_range = range(1, n_g)

    own_p = pltpu.make_async_copy(p_ref, p_all.at[0, r], local_sem.at[0])
    own_q = pltpu.make_async_copy(q_ref, q_all.at[0, z], local_sem.at[1])
    own_pos = pltpu.make_async_copy(pos_ref, pos_v, local_sem.at[2])
    own_p.start()
    own_q.start()
    own_pos.start()

    barrier = pltpu.get_barrier_semaphore()
    for device in [z_dev(d) for d in z_range] + [g_dev(d) for d in g_range]:
        pl.semaphore_signal(barrier, inc=1, device_id=device, device_id_type=MESH)
    pl.semaphore_wait(barrier, n_z - 1 + n_g - 1)

    q_copies = [copy(z_dev(d), q_ref, q_all.at[0, z], q_ss, q_rs, d) for d in z_range]
    p_copies = [copy(r_dev(d), p_ref, p_all.at[0, r], p_ss, p_rs, d) for d in r_range]
    p_shared = [copy(sibling, p_ref, p_all.at[1, r], pf_ss, pf_rs, 0)]
    for cp in p_copies + q_copies + p_shared:
        cp.start()

    own_p.wait()
    own_q.wait()
    own_pos.wait()
    q_own = q_all[0, z]
    p_own = p_all[0, r]
    slot = lax.broadcasted_iota(jnp.int32, (rows, rows), 0)
    onehot_t = jnp.where(slot == pos_v[...], 1.0, 0.0).astype(F32)
    paired_p = jnp.dot(onehot_t.T.astype(BF16), p_own, preferred_element_type=F32)
    pair_p[...] = paired_p
    pair_q[...] = jnp.dot(onehot_t.astype(BF16), q_own, preferred_element_type=F32)
    own_sum = logit_scale * jnp.sum(q_own.astype(F32) * paired_p, axis=(0, 1), keepdims=True)
    for d in r_range:
        p_copies[d - 1].wait_recv()
        at = r_at(n_row - d)
        cp = copy(sibling, p_all.at[0, at], p_all.at[1, at], pf_ss, pf_rs, d)
        cp.start()
        p_shared.append(cp)
    for cp in p_shared:
        cp.wait_recv()
    for cp in q_copies:
        cp.wait_recv()

    q_mat = q_all[0].reshape(half_q, width)
    p_mat = p_all[...].reshape(2 * half_p, width)
    s = logit_scale * lax.dot_general(q_mat, p_mat, NT, preferred_element_type=F32)

    s_t = logit_scale * lax.dot_general(p_mat, q_mat, NT, preferred_element_type=F32)

    def across(x, half):
        return (jnp.sum(x[:, :half], axis=1, keepdims=True)
                + jnp.sum(x[:, half:], axis=1, keepdims=True))

    row_peak = jnp.max(s_t, axis=0, keepdims=True)
    row_stat[z, 0:1, :] = row_peak
    row_stat[z, 1:2, :] = jnp.sum(jnp.exp(s_t - row_peak), axis=0, keepdims=True)
    row_stat[z, 2:3, :] = jnp.broadcast_to(own_sum, (1, half_q))
    rst = [copy(z_dev(d), row_stat.at[z], row_stat.at[z], rst_ss, rst_rs, d) for d in z_range]
    for cp in rst:
        cp.start()
    col_peak = jnp.max(s, axis=0, keepdims=True)
    col_exp = jnp.exp(s - col_peak)
    col_sum = jnp.sum(col_exp, axis=0, keepdims=True)
    col_stat[g, 0:1, :] = col_peak
    col_stat[g, 1:2, :] = col_sum
    col_swap[0:1, :half_p] = col_peak[:, half_p:]
    col_swap[0:1, half_p:] = col_peak[:, :half_p]
    col_swap[1:2, :half_p] = col_sum[:, half_p:]
    col_swap[1:2, half_p:] = col_sum[:, :half_p]
    cst = [copy(g_dev(d), col_swap if d % 2 else col_stat.at[g], col_stat.at[g], cst_ss, cst_rs, d)
           for d in g_range]
    for cp in cst:
        cp.start()
    q_shared = copy(sibling, q_all.at[0], q_all.at[1], qf_ss, qf_rs, 0)
    q_shared.start()
    for cp in cst + rst:
        cp.wait()

    def merge(ref):
        peak = ref[:, 0, :]
        total = ref[:, 1, :]
        top = jnp.max(peak, axis=0, keepdims=True)
        return top + jnp.log(jnp.sum(total * jnp.exp(peak - top), axis=0, keepdims=True))

    row_lse = merge(row_stat)
    col_lse = merge(col_stat)
    row_mat = jnp.broadcast_to(row_lse, (128, half_q)).T
    row_mat = jnp.concatenate([row_mat] * (2 * half_p // 128), axis=1)
    col_factor = 0.5 * jnp.exp(col_peak - col_lse)
    w = 0.5 * jnp.exp(s - row_mat) + col_exp * col_factor
    w_t = w.T.astype(BF16)
    w_sent[...] = w_t[half_p:]
    w_copy = copy(sibling, w_sent, w_got, w_ss, w_rs, 0)
    w_copy.start()

    dq = jnp.dot(w.astype(BF16), p_mat, preferred_element_type=F32).astype(BF16)
    dq_send[...] = dq.reshape(n_z, rows, width)
    dqc = [copy(z_dev(d), dq_send.at[z_at(d)], dq_recv.at[z], dq_ss, dq_rs, d) for d in z_range]
    for cp in dqc:
        cp.start()
    q_shared.wait()
    w_copy.wait()
    w_both = jnp.concatenate([w_t[:half_p], w_got[...]], axis=1)
    q_both = q_all[...].reshape(2 * half_q, width)
    dp = jnp.dot(w_both, q_both, preferred_element_type=F32).astype(BF16)
    dp_send[...] = dp.reshape(n_row, rows, width)
    dpc = [copy(r_dev(d), dp_send.at[r_at(d)], dp_recv.at[r], dp_ss, dp_rs, d) for d in r_range]
    for cp in dpc:
        cp.start()
    pos_row = jnp.sum(row_stat[:, 2, 0:1], axis=0, keepdims=True)
    loss_r[g] = jnp.broadcast_to(jnp.sum(row_lse, axis=1, keepdims=True) - 2.0 * pos_row, (8, 128))
    loss_z[z] = jnp.broadcast_to(across(col_lse, half_p), (8, 128))
    lrc = [copy(g_dev(d), loss_r.at[g], loss_r.at[g], lr_ss, lr_rs, d) for d in g_range]
    lzc = [copy(z_dev(d), loss_z.at[z], loss_z.at[z], lz_ss, lz_rs, d) for d in z_range]
    for cp in lrc + lzc:
        cp.start()
    dq_recv[z] = dq_send[z]
    dp_recv[r] = dp_send[r]
    for cp in q_copies + p_copies + p_shared:
        cp.wait_send()

    for cp in dpc:
        cp.wait()
    acc = dp_recv[0].astype(F32)
    for i in r_range:
        acc += dp_recv[i].astype(F32)
    gp_ref[...] = (logit_scale * (acc - pair_q[...])).astype(BF16)

    for cp in lrc + lzc:
        cp.wait()
    total = jnp.sum(loss_r[:, 0, 0:1], axis=0, keepdims=True) + jnp.sum(loss_z[:, 0, 0:1], axis=0, keepdims=True)
    loss_ref[...] = jnp.broadcast_to(total / (2.0 * rows * n_row * n_col), (8, 128))

    for cp in dqc:
        cp.wait()
    acc = dq_recv[0].astype(F32)
    for i in z_range:
        acc += dq_recv[i].astype(F32)
    gq_ref[...] = (logit_scale * (acc - pair_p[...])).astype(BF16)


def hand_out(loss_ref, gq_ref, gp_ref, loss_out, gq_out, gp_out, loss_v, sem):
    loss_v[...] = loss_ref[0:1, 0:1]
    pairs = ((gq_ref, gq_out), (gp_ref, gp_out), (loss_v, loss_out))
    copies = [pltpu.make_async_copy(src, dst, sem.at[i]) for i, (src, dst) in enumerate(pairs)]
    for cp in copies:
        cp.start()
    for cp in copies:
        cp.wait()


def local(n_row, n_col, query, passage, positive):
    rows, width = query.shape
    n_z, n_g = n_col // 2, n_row * 2
    dma = pltpu.SemaphoreType.DMA
    loss, gq, gp = pl.pallas_call(
        functools.partial(kernel, n_row, n_col),
        out_shape=(
            pltpu.VMEM((8, 128), F32),
            pltpu.VMEM((rows, width), BF16),
            pltpu.VMEM((rows, width), BF16),
        ),
        in_specs=[pl.BlockSpec(memory_space=pltpu.HBM)] * 3,
        out_specs=[pl.BlockSpec(memory_space=pltpu.VMEM)] * 3,
        scratch_shapes=[
            pltpu.VMEM((2, n_z, rows, width), BF16),
            pltpu.VMEM((2, n_row, rows, width), BF16),
            pltpu.VMEM((1, rows), jnp.int32),
            pltpu.VMEM((rows, width), F32),
            pltpu.VMEM((rows, width), F32),
            pltpu.VMEM((n_z, 8, n_z * rows), F32),
            pltpu.VMEM((n_g, 8, n_g * rows), F32),
            pltpu.VMEM((8, n_g * rows), F32),
            pltpu.VMEM((n_row * rows, n_z * rows), BF16),
            pltpu.VMEM((n_row * rows, n_z * rows), BF16),
            pltpu.VMEM((n_z, rows, width), BF16),
            pltpu.VMEM((n_row, rows, width), BF16),
            pltpu.VMEM((n_z, rows, width), BF16),
            pltpu.VMEM((n_row, rows, width), BF16),
            pltpu.VMEM((n_g, 8, 128), F32),
            pltpu.VMEM((n_z, 8, 128), F32),
            dma((3,)),
            dma((n_z,)), dma((n_z,)), dma((n_row,)), dma((n_row,)),
            dma((1,)), dma((1,)), dma((n_row,)), dma((n_row,)),
            dma((1,)), dma((1,)),
            dma((n_z,)), dma((n_z,)), dma((n_g,)), dma((n_g,)),
            dma((n_z,)), dma((n_z,)), dma((n_row,)), dma((n_row,)),
            dma((n_g,)), dma((n_g,)), dma((n_z,)), dma((n_z,)),
        ],
        compiler_params=pltpu.CompilerParams(
            collective_id=0, has_side_effects=True, vmem_limit_bytes=48 * 1024 * 1024),
    )(*(pltpu.with_memory_space_constraint(x, pltpu.HBM) for x in (query, passage, positive)))
    loss, gq, gp = pl.pallas_call(
        hand_out,
        out_shape=(
            jax.ShapeDtypeStruct((1, 1), F32),
            jax.ShapeDtypeStruct(gq.shape, BF16),
            jax.ShapeDtypeStruct(gp.shape, BF16),
        ),
        in_specs=[pl.BlockSpec(memory_space=pltpu.VMEM)] * 3,
        out_specs=[pl.BlockSpec(memory_space=pl.ANY)] * 3,
        scratch_shapes=[pltpu.VMEM((1, 1), F32), dma((3,))],
    )(*(pltpu.with_memory_space_constraint(x, pltpu.VMEM) for x in (loss, gq, gp)))
    return loss[0, 0], gq, gp


def solution(mesh):
    return jax.shard_map(
        functools.partial(local, mesh.shape["row"], mesh.shape["col"]),
        mesh=mesh,
        in_specs=(P(("row", "col"), None), P(("row", "col"), None), P(("row", "col"), None)),
        out_specs=(P(), P(("row", "col"), None), P(("row", "col"), None)),
        check_vma=False,
    )
```
